256 devices in a mesh: group: 8 (over z), block: 32 (over x, y, core).
Axes of the slice: x: 4, y: 4, z: 8, core: 2. Of those that a mesh axis runs over, the one named last changes fastest.
Arguments:
- jacobians: bfloat16 [3072, 128, 1152], P(('group', 'block')), may hold values from -0.15625 to 0.15625
- destination: int32 [3072], P(('group', 'block')), may hold values from 0 to 31, as said below
- other_group: int32 [3072], P(('group', 'block')), may hold values from 0 to 7, as said below
- live_rows: int32 [3072], P(('group', 'block')), may hold values from 64 to 128, as said below
- damping: float32 [256, 576], P(('group', 'block')), may hold values from 0.5 to 2
- right_side: float32 [256, 576], P(('group', 'block')), may hold values from -18 to 18
Outputs:
- solution: float32 [256, 576], P(('group', 'block'))
- residual: float32 [256, 576], P(('group', 'block'))
The draws below stay inside these ranges and needn't reach their ends.
Inputs may be any that keep to these rules, and one draw needn't show every extreme that they name: `destination`: the observation blocks of one device name any one camera block at most 2 times; in every group some camera block is named exactly 2 times by every device of that group. `other_group`: an observation block's covisible group differs from the group of the device that holds it. `live_rows`: every device holds a block whose 128 rows are all live.
All inputs are finite; a program needn't handle non-finite values.
Results may differ from the reference program's by a relative error of at most 0.009.
Values may be sent and summed in bfloat16 or wider, within the bound.
A program may use at most 128 MiB of HBM per device.

```python
import math
import jax
import jax.numpy as jnp
from jax import lax

PARAMS = 576
ROWS = 128
OBS_DEV = 12
ITERS = 2
OWNERS = 32
GROUPS = 8
CAP = 2
CAMS = 256
GROUP_BLOCKS = 384
BLOCKS_ALL = 3072


def draw_destination(key, part):
    base_key = jax.random.fold_in(key, 101)
    hot_key, pick_key, order_key = jax.random.split(base_key, 3)
    hot_owner = jax.random.randint(hot_key, (GROUPS,), 0, OWNERS)
    device_hot = jnp.repeat(hot_owner, OWNERS)
    spare_slots = (OWNERS - 1) * CAP
    picked = jax.vmap(lambda subkey: jax.random.permutation(subkey, spare_slots))(jax.random.split(pick_key, CAMS))
    picked = picked[:, :OBS_DEV - CAP].astype(jnp.int32)
    shifted = picked // CAP
    others = shifted + (shifted >= device_hot[:, None]).astype(jnp.int32)
    hot_part = jnp.broadcast_to(device_hot[:, None], (CAMS, CAP)).astype(jnp.int32)
    listed = jnp.concatenate([hot_part, others], axis=1)
    orders = jax.vmap(lambda subkey: jax.random.permutation(subkey, OBS_DEV))(jax.random.split(order_key, CAMS))
    mixed = jnp.take_along_axis(listed, orders.astype(jnp.int32), axis=1)
    return mixed.reshape(BLOCKS_ALL).astype(jnp.int32)


def draw_other_group(key, part):
    position = jnp.arange(BLOCKS_ALL, dtype=jnp.int32)
    own_group = position // GROUP_BLOCKS
    offset = jax.random.randint(jax.random.fold_in(key, 202), (BLOCKS_ALL,), 1, GROUPS)
    return ((own_group + offset) % GROUPS).astype(jnp.int32)


def draw_live_rows(key, part):
    count_key, full_key = jax.random.split(jax.random.fold_in(key, 303))
    counts = jax.random.randint(count_key, (CAMS, OBS_DEV), ROWS // 2, ROWS + 1)
    full_at = jax.random.randint(full_key, (CAMS, 1), 0, OBS_DEV)
    column = jnp.arange(OBS_DEV, dtype=jnp.int32)[None, :]
    counts = jnp.where(column == full_at, ROWS, counts)
    return counts.reshape(BLOCKS_ALL).astype(jnp.int32)


def draw_right_side(key, part):
    value_key = jax.random.fold_in(jax.random.fold_in(key, 404), 0)
    ramp = 1.0 + 2.0 * jnp.arange(CAMS, dtype=jnp.float32) / (CAMS - 1)
    values = jnp.clip(jax.random.normal(value_key, (CAMS, PARAMS), jnp.float32), -6.0, 6.0)
    return (values * ramp[:, None]).astype(jnp.float32)


def level_of(rng, dims, cuts, low, top_value):
    level, own = 1.0, jax.random.fold_in(rng, 6)
    for axis_at, shards_of in cuts:
        draws = jnp.exp(jax.random.uniform(jax.random.fold_in(own, axis_at), (shards_of,), jnp.float32, low / len(cuts), top_value / len(cuts)))
        level = level * jnp.repeat(draws, dims[axis_at] // shards_of).reshape([-1 if axis == axis_at else 1 for axis in range(len(dims))])
    return level


def normal_values(rng, extent, deviation, most, cuts=(), held_as=jnp.bfloat16):
    drawn = deviation * jax.random.normal(rng, extent, jnp.float32)
    if cuts:
        drawn = drawn * level_of(rng, extent, cuts, -0.22, 0.18)
    return jnp.clip(drawn, -most, most).astype(held_as)


def setup_inputs(seed: int = 0) -> dict:
    streams_of = jax.random.split(jax.random.key(seed), 7)
    return {
        "jacobians": normal_values(streams_of[0], (BLOCKS_ALL, ROWS, 2 * PARAMS), (ROWS * OBS_DEV) ** -0.5, 0.15625, ((0, 256),)),
        "destination": draw_destination(jax.random.fold_in(streams_of[6], 71), 0),
        "other_group": draw_other_group(jax.random.fold_in(streams_of[6], 71), 0),
        "live_rows": draw_live_rows(jax.random.fold_in(streams_of[6], 71), 0),
        "damping": jnp.clip(jnp.exp(math.log(2.0) - 1.3862944 * jax.random.uniform(streams_of[4], (CAMS, PARAMS), jnp.float32) ** level_of(streams_of[4], (CAMS, PARAMS), ((0, 256),), -0.2, 0.2)), 0.5, 2.0),
        "right_side": draw_right_side(jax.random.fold_in(streams_of[6], 71), 0),
    }


def camera_indices(destination, other_group):
    position = jnp.arange(BLOCKS_ALL, dtype=jnp.int32)
    home_index = (position // GROUP_BLOCKS).astype(jnp.int32) * OWNERS + destination
    other_index = other_group * OWNERS + destination
    return home_index, other_index


def mask_rows(blocks, live_part):
    row_index = jnp.arange(ROWS, dtype=jnp.int32)
    keep = row_index[None, :, None] < live_part[:, None, None]
    return jnp.where(keep, blocks, jnp.zeros_like(blocks))


def accumulate(jacobians, live_rows, home_index, other_index, make_terms):
    pieces = (jacobians.reshape(CAMS, OBS_DEV, ROWS, 2 * PARAMS), live_rows.reshape(CAMS, OBS_DEV),
              home_index.reshape(CAMS, OBS_DEV), other_index.reshape(CAMS, OBS_DEV))

    def advance(running_sum, piece):
        blocks, live_part, home_part, other_part = piece
        kept_blocks = mask_rows(blocks, live_part).astype(jnp.float32)
        term_rows = make_terms(kept_blocks, home_part, other_part)
        running_sum = running_sum.at[home_part].add(term_rows[:, :PARAMS])
        running_sum = running_sum.at[other_part].add(term_rows[:, PARAMS:])
        return running_sum, None

    start = jnp.zeros((CAMS, PARAMS), jnp.float32)
    result, unused = lax.scan(advance, start, pieces)
    return result


def reference(jacobians, destination, other_group, live_rows, damping, right_side):
    home_index, other_index = camera_indices(destination, other_group)

    def square_terms(kept_blocks, home_part, other_part):
        return jnp.sum(kept_blocks * kept_blocks, axis=1)

    diagonal_sum = damping + accumulate(jacobians, live_rows, home_index, other_index, square_terms)

    def operate(vector):
        low_field = lax.optimization_barrier(vector.astype(jnp.bfloat16))

        def product_terms(kept_blocks, home_part, other_part):
            inputs = jnp.concatenate([low_field[home_part], low_field[other_part]], axis=1).astype(jnp.float32)
            projected = jnp.einsum("nrc,nc->nr", kept_blocks, inputs, precision=lax.Precision.HIGHEST)
            projected = lax.optimization_barrier(projected.astype(jnp.bfloat16)).astype(jnp.float32)
            return jnp.einsum("nrc,nr->nc", kept_blocks, projected, precision=lax.Precision.HIGHEST)

        return damping * vector + accumulate(jacobians, live_rows, home_index, other_index, product_terms)

    solution = jnp.zeros((CAMS, PARAMS), jnp.float32)
    residual = right_side
    scaled_res = residual / diagonal_sum
    direction = scaled_res
    precond_norm = jnp.sum(residual * scaled_res)
    for iteration in range(ITERS):
        operator_image = operate(direction)
        step_size = precond_norm / jnp.sum(direction * operator_image)
        solution = solution + step_size * direction
        residual = residual - step_size * operator_image
        if iteration + 1 < ITERS:
            scaled_res = residual / diagonal_sum
            next_norm = jnp.sum(residual * scaled_res)
            direction = scaled_res + (next_norm / precond_norm) * direction
            precond_norm = next_norm
    return solution, residual
```

```python
import functools

import jax
import jax.numpy as jnp
from jax import lax
from jax.experimental import pallas as pl
from jax.experimental.pallas import tpu as pltpu
from jax.sharding import PartitionSpec as P

LANES = 128
MSG = 16
F32 = jnp.float32
BF16 = jnp.bfloat16


def total(value):
    return jnp.sum(jnp.sum(value, axis=1, keepdims=True), axis=0, keepdims=True)


def iota(shape, dim):
    return lax.broadcasted_iota(jnp.int32, shape, dim)


def dot(left, right, contract=((1,), (0,))):
    return lax.dot_general(left, right, (contract, ((), ())), preferred_element_type=F32)


def cg_kernel(
    groups, owners, count, rows, params,
    jac_hbm, dest_ref, other_ref, live_ref, damp_ref, rhs_ref,
    sol_ref, res_ref,
    jac, pack, unpack, snd, rcv, ctx, wide, row_snd, row_rcv,
    jac_sem, snd_sem, rcv_sem, zsnd_sem, zrcv_sem,
):
    me_g = lax.axis_index("group")
    me_b = lax.axis_index("block")
    width = jac.shape[1]
    tiles = (params + LANES - 1) // LANES
    padded = tiles * LANES
    kpad = 16

    def block_copy(k):
        part = pl.ds(k * rows, rows)
        return pltpu.make_async_copy(jac_hbm.at[part], jac.at[part], jac_sem.at[k])

    for k in range(count):
        block_copy(k).start()

    barrier = pltpu.get_barrier_semaphore()

    def greet_block(step, carry):
        peer = (me_b + step) % owners
        pl.semaphore_signal(
            barrier, inc=1, device_id=(me_g, peer), device_id_type=pl.DeviceIdType.MESH
        )
        return carry

    def greet_group(step, carry):
        peer = (me_g + step) % groups
        pl.semaphore_signal(
            barrier, inc=1, device_id=(peer, me_b), device_id_type=pl.DeviceIdType.MESH
        )
        return carry

    lax.fori_loop(1, owners, greet_block, 0)
    lax.fori_loop(1, groups, greet_group, 0)

    def own_part():
        return pl.ds(pl.multiple_of(me_b * MSG, MSG), MSG)

    def block_send(stage):
        def body(step, carry):
            peer = (me_b + step) % owners
            pltpu.make_async_remote_copy(
                src_ref=snd.at[stage, pl.ds(pl.multiple_of(peer * MSG, MSG), MSG)],
                dst_ref=rcv.at[stage, own_part()],
                send_sem=snd_sem.at[stage],
                recv_sem=rcv_sem.at[stage],
                device_id=(me_g, peer),
                device_id_type=pl.DeviceIdType.MESH,
            ).start()
            return carry

        lax.fori_loop(1, owners, body, 0)
        rcv[stage, own_part()] = snd[stage, own_part()]

    def block_wait(ref, sem, stage):
        part = ref.at[stage, pl.ds(0, (owners - 1) * MSG)]
        pltpu.make_async_copy(part, part, sem.at[stage]).wait()

    def group_send(stage, src_of, dst):
        def body(step, carry):
            peer = (me_g + step) % groups
            pltpu.make_async_remote_copy(
                src_ref=src_of(peer),
                dst_ref=dst,
                send_sem=zsnd_sem.at[stage],
                recv_sem=zrcv_sem.at[stage],
                device_id=(peer, me_b),
                device_id_type=pl.DeviceIdType.MESH,
            ).start()
            return carry

        lax.fori_loop(1, groups, body, 0)

    def group_wait(part, sem, stage):
        pltpu.make_async_copy(part, part, sem.at[stage]).wait()

    sub = iota((kpad, LANES), 0)
    lane = iota((kpad, LANES), 1)
    dest_col = jnp.full((kpad, LANES), -1, jnp.int32)
    dest_row = jnp.full((kpad, LANES), -1, jnp.int32)
    live_col = jnp.zeros((kpad, LANES), jnp.int32)
    other_col = jnp.zeros((kpad, LANES), jnp.int32)
    for k in range(count):
        dest_col = jnp.where(sub == k, dest_ref[k], dest_col)
        dest_row = jnp.where(lane == k, dest_ref[k], dest_row)
        live_col = jnp.where(sub == k, live_ref[k], live_col)
        other_col = jnp.where(sub == k, other_ref[k], other_col)
    same = jnp.where((dest_col == dest_row) & (dest_row >= 0), 1.0, 0.0)
    rank_row = jnp.sum(jnp.where(sub < lane, same, 0.0), axis=0, keepdims=True)
    rank_col = jnp.sum(jnp.where(lane < sub, same, 0.0), axis=1, keepdims=True)
    slot = iota((3 * owners, LANES), 0)
    dest_rows = jnp.broadcast_to(dest_row[:1], (3 * owners, LANES))
    rank_rows = jnp.broadcast_to(rank_row, (3 * owners, LANES))
    slot_hit = dest_rows == slot % owners
    slot_rank = (slot // owners - 1).astype(F32)
    to_slot = jnp.where(slot_hit & ((slot < owners) | (rank_rows == slot_rank)), 1.0, 0.0)
    to_slot = to_slot[:, :kpad].astype(BF16)
    slot_lane = iota((kpad, LANES), 1)
    lane_hit = dest_col == slot_lane % owners
    lane_rank = (slot_lane // owners - 1).astype(F32)
    rank_cols = jnp.broadcast_to(rank_col, (kpad, LANES))
    from_home = jnp.where(lane_hit & (slot_lane < owners), 1.0, 0.0).astype(BF16)
    from_far = jnp.where(
        lane_hit & (slot_lane >= owners) & (rank_cols == lane_rank), 1.0, 0.0
    ).astype(BF16)
    keep = jnp.concatenate(
        [jnp.where((sub == k) & (lane < live_col), 1.0, 0.0) for k in range(count)], axis=1
    )
    panel_lane = iota((kpad, padded), 1)

    def put_rows(first, value):
        for c in range(tiles):
            pack[pl.ds(first + c, owners, stride=MSG), :] = value[:, c * LANES : (c + 1) * LANES]

    def put_message(stage, home, far_a, far_b, last):
        put_rows(0, home)
        put_rows(tiles, far_a)
        put_rows(2 * tiles, far_b)
        pack[pl.ds(3 * tiles, owners, stride=MSG), :] = last
        snd[stage] = pack[...].astype(BF16)
        block_send(stage)

    def send_terms(stage, terms, last):
        home = jnp.where(panel_lane < params, terms[:, :padded], 0.0)
        far = jnp.where(panel_lane < params, pltpu.roll(terms, params, 1)[:, :padded], 0.0)
        high = home.astype(BF16)
        low = (home - high.astype(F32)).astype(BF16)
        home_out = dot(to_slot[:owners], high) + dot(to_slot[:owners], low)
        far_out = dot(to_slot[owners:], far.astype(BF16))
        put_message(stage, home_out, far_out[:owners], far_out[owners:], last)

    def get_message(stage):
        block_wait(rcv, rcv_sem, stage)
        unpack[...] = rcv[stage].astype(F32)

        def row(c):
            return unpack[pl.ds(c, owners, stride=MSG), :]

        parts = [
            jnp.concatenate([row(s * tiles + c) for c in range(tiles)], axis=1) for s in range(3)
        ]
        return jnp.concatenate(parts, axis=0).astype(BF16), row(3 * tiles)

    last_lane = iota((owners, LANES), 1)

    def split(value, first):
        high = value.astype(BF16).astype(F32)
        middle = (value - high).astype(BF16).astype(F32)
        low = value - high - middle
        out = jnp.where(last_lane == first, jnp.broadcast_to(high, last_lane.shape), 0.0)
        out = out + jnp.where(last_lane == first + 1, jnp.broadcast_to(middle, last_lane.shape), 0.0)
        return out + jnp.where(last_lane == first + 2, jnp.broadcast_to(low, last_lane.shape), 0.0)

    wide_lane = iota((groups, padded), 1)
    wide_row = iota((groups, padded), 0)
    pl.semaphore_wait(barrier, owners - 1 + groups - 1)
    ctx[me_g] = jnp.zeros((2, padded), F32)
    ctx[me_g, 0:1, 0:params] = damp_ref[...]
    ctx[me_g, 1:2, 0:params] = rhs_ref[...]
    group_send(0, lambda peer: ctx.at[me_g], ctx.at[me_g])

    sum_rows = []
    for k in range(count):
        block_copy(k).wait()
        block = jac[k * rows : (k + 1) * rows, :].astype(F32)
        live = iota((rows, width), 0) < live_ref[k]
        kept = jnp.where(live, block, 0.0)
        sum_rows.append(jnp.sum(kept * kept, axis=0, keepdims=True))
    sum_rows += [jnp.zeros((1, width), F32)] * (kpad - count)
    squares = jnp.concatenate(sum_rows, axis=0)
    others = jnp.where(sub < count, other_col, 0).astype(F32).astype(BF16)
    other_out = dot(to_slot[owners:], others)
    send_terms(
        0, squares, jnp.where(last_lane < LANES // 2, other_out[:owners], other_out[owners:])
    )
    got, ids = get_message(0)
    group_col = iota((owners, LANES), 1).astype(F32)
    id_a = jnp.broadcast_to(ids[:, :1], (owners, LANES))
    id_b = jnp.broadcast_to(ids[:, LANES // 2 : LANES // 2 + 1], (owners, LANES))
    select = jnp.concatenate(
        [
            jnp.where(group_col == me_g.astype(F32), 1.0, 0.0),
            jnp.where(group_col == id_a, 1.0, 0.0),
            jnp.where(group_col == id_b, 1.0, 0.0),
        ],
        axis=0,
    )
    if 3 * owners < LANES:
        select_t = jnp.concatenate([select, jnp.zeros((LANES - 3 * owners, LANES), F32)], axis=0).T
    else:
        select_t = select.T
    select = select[:, :kpad].astype(BF16)
    select_t = select_t[:kpad, : 3 * owners].astype(BF16)

    def sum_over_groups(stage, got, scalar):
        panel = dot(select_t, got)[:groups]
        if scalar is not None:
            spot = (wide_row == 0) & (wide_lane == params)
            panel = jnp.where(spot, jnp.broadcast_to(scalar, panel.shape), panel)
        wide[stage, me_g] = panel
        group_send(1 + stage, lambda peer: wide.at[stage, me_g], wide.at[stage, me_g])
        group_wait(wide.at[stage, pl.ds(0, groups - 1)], zrcv_sem, 1 + stage)
        out = wide[stage, 0]
        for g in range(1, groups):
            out = out + wide[stage, g]
        return jnp.where(wide_lane < params, out, 0.0), total(jnp.where(wide_lane < params, 0.0, out))

    def send_panel(stage, panel, last):
        low = jnp.concatenate([panel, jnp.zeros((kpad - groups, padded), F32)], axis=0)
        out = dot(select, low.astype(BF16))
        put_message(stage, out[:owners], out[owners : 2 * owners], out[2 * owners :], last)

    def inputs_of(got):
        home = dot(from_home[:, :owners], got[:owners])
        far = dot(from_far[:, owners : 3 * owners], got[owners:])
        fill = jnp.zeros((kpad, width - padded), F32)
        home = jnp.concatenate([home, fill], axis=1)
        far = pltpu.roll(jnp.concatenate([far, fill], axis=1), params, 1)
        return (home + far).astype(BF16)

    def own_row(panel):
        return jnp.sum(jnp.where(wide_row == me_g, panel, 0.0), axis=0, keepdims=True)

    summed, unused = sum_over_groups(0, got, None)
    group_wait(ctx.at[pl.ds(0, groups - 1)], zrcv_sem, 0)
    damping = jnp.concatenate([ctx[g, 0:1, :] for g in range(groups)], axis=0)
    right_side = jnp.concatenate([ctx[g, 1:2, :] for g in range(groups)], axis=0)
    diagonal = jnp.where(wide_lane < params, damping + summed, 1.0)
    direction = right_side / diagonal

    send_panel(
        1,
        direction,
        split(total(right_side * direction), 0)
        + split(total(damping * direction * direction), LANES // 2),
    )
    got, scalars = get_message(1)
    norm = total(jnp.where(last_lane < LANES // 2, scalars, 0.0))
    damped = total(jnp.where(last_lane < LANES // 2, 0.0, scalars))
    product = dot(inputs_of(got), jac[...], ((1,), (1,)))
    kept = product * keep
    projected = kept.astype(BF16)
    returned = dot(projected, jac[...])
    send_terms(2, returned, split(total(kept * projected.astype(F32)), 0))
    got, scalars = get_message(2)
    summed, square = sum_over_groups(1, got, total(scalars))
    step_size = norm / (damped + square)
    residual = right_side - step_size * (damping * direction + summed)
    scaled = residual / diagonal

    send_panel(3, scaled, split(total(residual * scaled), 0))
    got, scalars = get_message(3)
    next_norm = total(scalars)
    beta = next_norm / norm
    product = dot(inputs_of(got), jac[...], ((1,), (1,))) + beta * product
    kept = product * keep
    projected = kept.astype(BF16)
    returned = dot(projected, jac[...])
    first_direction = own_row(direction)
    own_damping = own_row(damping)
    next_direction = own_row(scaled) + beta * first_direction
    partial = total(kept * projected.astype(F32)) + total(
        own_damping * next_direction * next_direction
    )
    send_terms(4, returned, split(partial, 0))
    got, scalars = get_message(4)
    panel = dot(select_t, got)[:groups]
    panel = jnp.where(wide_lane == params, jnp.broadcast_to(total(scalars), panel.shape), panel)
    for g in range(groups):
        row_snd[g] = panel[g : g + 1]
    row_rcv[me_g] = own_row(panel)
    group_send(3, lambda peer: row_snd.at[peer], row_rcv.at[me_g])
    group_wait(row_rcv.at[pl.ds(0, groups - 1)], zrcv_sem, 3)
    out = row_rcv[0]
    for g in range(1, groups):
        out = out + row_rcv[g]
    one_lane = iota((1, padded), 1)
    curvature = total(jnp.where(one_lane == params, out, 0.0))
    next_step = next_norm / curvature
    image = own_damping * next_direction + out
    sol_ref[...] = (step_size * first_direction + next_step * next_direction)[:, :params]
    res_ref[...] = (own_row(residual) - next_step * image)[:, :params]

    for stage in range(5):
        block_wait(snd, snd_sem, stage)
    group_wait(ctx.at[pl.ds(0, groups - 1)], zsnd_sem, 0)
    for stage in range(2):
        group_wait(wide.at[stage, pl.ds(0, groups - 1)], zsnd_sem, 1 + stage)
    group_wait(row_snd.at[pl.ds(0, groups - 1)], zsnd_sem, 3)


def on_device(groups, owners, jacobians, destination, other_group, live_rows, damping, right_side):
    count, rows, width = jacobians.shape
    params = width // 2
    padded = (params + LANES - 1) // LANES * LANES
    vmem = pl.BlockSpec(memory_space=pltpu.VMEM)
    smem = pl.BlockSpec(memory_space=pltpu.SMEM)
    return pl.pallas_call(
        functools.partial(cg_kernel, groups, owners, count, rows, params),
        out_shape=(
            jax.ShapeDtypeStruct(right_side.shape, F32),
            jax.ShapeDtypeStruct(right_side.shape, F32),
        ),
        in_specs=[pl.BlockSpec(memory_space=pl.ANY), smem, smem, smem, vmem, vmem],
        out_specs=(vmem, vmem),
        scratch_shapes=[
            pltpu.VMEM((count * rows, width), BF16),
            pltpu.VMEM((owners * MSG, LANES), F32),
            pltpu.VMEM((owners * MSG, LANES), F32),
            pltpu.VMEM((5, owners * MSG, LANES), BF16),
            pltpu.VMEM((5, owners * MSG, LANES), BF16),
            pltpu.VMEM((groups, 2, padded), F32),
            pltpu.VMEM((2, groups, groups, padded), F32),
            pltpu.VMEM((groups, 1, padded), F32),
            pltpu.VMEM((groups, 1, padded), F32),
            pltpu.SemaphoreType.DMA((count,)),
            pltpu.SemaphoreType.DMA((5,)),
            pltpu.SemaphoreType.DMA((5,)),
            pltpu.SemaphoreType.DMA((4,)),
            pltpu.SemaphoreType.DMA((4,)),
        ],
        compiler_params=pltpu.CompilerParams(
            collective_id=0, has_side_effects=True, vmem_limit_bytes=40 * 1024 * 1024
        ),
    )(
        jacobians.reshape(count * rows, width), destination, other_group, live_rows, damping, right_side
    )


def solution(mesh):
    placed = (
        P(("group", "block"), None, None),
        P(("group", "block")),
        P(("group", "block")),
        P(("group", "block")),
        P(("group", "block"), None),
        P(("group", "block"), None),
    )
    return jax.shard_map(
        functools.partial(on_device, mesh.shape["group"], mesh.shape["block"]),
        mesh=mesh,
        in_specs=placed,
        out_specs=(P(("group", "block"), None), P(("group", "block"), None)),
        check_vma=False,
    )
```

```python
import functools

import jax
import jax.numpy as jnp
from jax import lax
from jax.experimental import pallas as pl
from jax.experimental.pallas import tpu as pltpu
from jax.sharding import PartitionSpec as P

LANES = 128
MSG = 16
F32 = jnp.float32
BF16 = jnp.bfloat16


def total(value):
    return jnp.sum(jnp.sum(value, axis=1, keepdims=True), axis=0, keepdims=True)


def iota(shape, dim):
    return lax.broadcasted_iota(jnp.int32, shape, dim)


def dot(left, right, contract=((1,), (0,))):
    return lax.dot_general(left, right, (contract, ((), ())), preferred_element_type=F32)


def cg_kernel(
    groups, owners, count, rows, params,
    jac_hbm, dest_hbm, other_hbm, live_hbm, damp_hbm, rhs_hbm,
    sol_ref, res_ref,
    jac, dest_ref, other_ref, live_ref, damp_ref, rhs_ref,
    pack, unpack, snd, rcv, ctx, wide, row_snd, row_rcv,
    jac_sem, in_sem, snd_sem, rcv_sem, zsnd_sem, zrcv_sem,
):
    me_g = lax.axis_index("group")
    me_b = lax.axis_index("block")
    width = jac.shape[1]
    tiles = (params + LANES - 1) // LANES
    padded = tiles * LANES
    kpad = 16

    def block_copy(k):
        part = pl.ds(k * rows, rows)
        return pltpu.make_async_copy(jac_hbm.at[part], jac.at[part], jac_sem.at[k])

    small = [
        pltpu.make_async_copy(source, target, in_sem.at[i])
        for i, (source, target) in enumerate(
            [
                (dest_hbm, dest_ref),
                (other_hbm, other_ref),
                (live_hbm, live_ref),
                (damp_hbm, damp_ref),
                (rhs_hbm, rhs_ref),
            ]
        )
    ]
    for copy in small:
        copy.start()
    for k in range(count):
        block_copy(k).start()

    barrier = pltpu.get_barrier_semaphore()

    def greet_block(step, carry):
        peer = (me_b + step) % owners
        pl.semaphore_signal(
            barrier, inc=1, device_id=(me_g, peer), device_id_type=pl.DeviceIdType.MESH
        )
        return carry

    def greet_group(step, carry):
        peer = (me_g + step) % groups
        pl.semaphore_signal(
            barrier, inc=1, device_id=(peer, me_b), device_id_type=pl.DeviceIdType.MESH
        )
        return carry

    lax.fori_loop(1, owners, greet_block, 0)
    lax.fori_loop(1, groups, greet_group, 0)

    def own_part():
        return pl.ds(pl.multiple_of(me_b * MSG, MSG), MSG)

    def block_send(stage):
        def body(step, carry):
            peer = (me_b + step) % owners
            pltpu.make_async_remote_copy(
                src_ref=snd.at[stage, pl.ds(pl.multiple_of(peer * MSG, MSG), MSG)],
                dst_ref=rcv.at[stage, own_part()],
                send_sem=snd_sem.at[stage],
                recv_sem=rcv_sem.at[stage],
                device_id=(me_g, peer),
                device_id_type=pl.DeviceIdType.MESH,
            ).start()
            return carry

        lax.fori_loop(1, owners, body, 0)
        rcv[stage, own_part()] = snd[stage, own_part()]

    def block_wait(ref, sem, stage):
        part = ref.at[stage, pl.ds(0, (owners - 1) * MSG)]
        pltpu.make_async_copy(part, part, sem.at[stage]).wait()

    def group_send(stage, src_of, dst):
        def body(step, carry):
            peer = (me_g + step) % groups
            pltpu.make_async_remote_copy(
                src_ref=src_of(peer),
                dst_ref=dst,
                send_sem=zsnd_sem.at[stage],
                recv_sem=zrcv_sem.at[stage],
                device_id=(peer, me_b),
                device_id_type=pl.DeviceIdType.MESH,
            ).start()
            return carry

        lax.fori_loop(1, groups, body, 0)

    def group_wait(part, sem, stage):
        pltpu.make_async_copy(part, part, sem.at[stage]).wait()

    for copy in small:
        copy.wait()

    sub = iota((kpad, LANES), 0)
    lane = iota((kpad, LANES), 1)
    dest_col = jnp.full((kpad, LANES), -1, jnp.int32)
    dest_row = jnp.full((kpad, LANES), -1, jnp.int32)
    live_col = jnp.zeros((kpad, LANES), jnp.int32)
    other_col = jnp.zeros((kpad, LANES), jnp.int32)
    for k in range(count):
        dest_col = jnp.where(sub == k, dest_ref[k], dest_col)
        dest_row = jnp.where(lane == k, dest_ref[k], dest_row)
        live_col = jnp.where(sub == k, live_ref[k], live_col)
        other_col = jnp.where(sub == k, other_ref[k], other_col)
    same = jnp.where((dest_col == dest_row) & (dest_row >= 0), 1.0, 0.0)
    rank_row = jnp.sum(jnp.where(sub < lane, same, 0.0), axis=0, keepdims=True)
    rank_col = jnp.sum(jnp.where(lane < sub, same, 0.0), axis=1, keepdims=True)
    slot = iota((3 * owners, LANES), 0)
    dest_rows = jnp.broadcast_to(dest_row[:1], (3 * owners, LANES))
    rank_rows = jnp.broadcast_to(rank_row, (3 * owners, LANES))
    slot_hit = dest_rows == slot % owners
    slot_rank = (slot // owners - 1).astype(F32)
    to_slot = jnp.where(slot_hit & ((slot < owners) | (rank_rows == slot_rank)), 1.0, 0.0)
    to_slot = to_slot[:, :kpad].astype(BF16)
    slot_lane = iota((kpad, LANES), 1)
    lane_hit = dest_col == slot_lane % owners
    lane_rank = (slot_lane // owners - 1).astype(F32)
    rank_cols = jnp.broadcast_to(rank_col, (kpad, LANES))
    from_home = jnp.where(lane_hit & (slot_lane < owners), 1.0, 0.0).astype(BF16)
    from_far = jnp.where(
        lane_hit & (slot_lane >= owners) & (rank_cols == lane_rank), 1.0, 0.0
    ).astype(BF16)
    keep = jnp.concatenate(
        [jnp.where((sub == k) & (lane < live_col), 1.0, 0.0) for k in range(count)], axis=1
    )
    panel_lane = iota((kpad, padded), 1)

    def put_rows(first, value):
        for c in range(tiles):
            pack[pl.ds(first + c, owners, stride=MSG), :] = value[:, c * LANES : (c + 1) * LANES]

    def put_message(stage, home, far_a, far_b, last):
        put_rows(0, home)
        put_rows(tiles, far_a)
        put_rows(2 * tiles, far_b)
        pack[pl.ds(3 * tiles, owners, stride=MSG), :] = last
        snd[stage] = pack[...].astype(BF16)
        block_send(stage)

    def send_terms(stage, terms, last):
        home = jnp.where(panel_lane < params, terms[:, :padded], 0.0)
        far = jnp.where(panel_lane < params, pltpu.roll(terms, params, 1)[:, :padded], 0.0)
        high = home.astype(BF16)
        low = (home - high.astype(F32)).astype(BF16)
        home_out = dot(to_slot[:owners], high) + dot(to_slot[:owners], low)
        far_out = dot(to_slot[owners:], far.astype(BF16))
        put_message(stage, home_out, far_out[:owners], far_out[owners:], last)

    def get_message(stage):
        block_wait(rcv, rcv_sem, stage)
        unpack[...] = rcv[stage].astype(F32)

        def row(c):
            return unpack[pl.ds(c, owners, stride=MSG), :]

        parts = [
            jnp.concatenate([row(s * tiles + c) for c in range(tiles)], axis=1) for s in range(3)
        ]
        return jnp.concatenate(parts, axis=0).astype(BF16), row(3 * tiles)

    last_lane = iota((owners, LANES), 1)

    def split(value, first):
        high = value.astype(BF16).astype(F32)
        middle = (value - high).astype(BF16).astype(F32)
        low = value - high - middle
        out = jnp.where(last_lane == first, jnp.broadcast_to(high, last_lane.shape), 0.0)
        out = out + jnp.where(last_lane == first + 1, jnp.broadcast_to(middle, last_lane.shape), 0.0)
        return out + jnp.where(last_lane == first + 2, jnp.broadcast_to(low, last_lane.shape), 0.0)

    wide_lane = iota((groups, padded), 1)
    wide_row = iota((groups, padded), 0)
    sum_rows = []
    for k in range(count):
        block_copy(k).wait()
        block = jac[k * rows : (k + 1) * rows, :].astype(F32)
        live = iota((rows, width), 0) < live_ref[k]
        kept = jnp.where(live, block, 0.0)
        sum_rows.append(jnp.sum(kept * kept, axis=0, keepdims=True))
    sum_rows += [jnp.zeros((1, width), F32)] * (kpad - count)
    squares = jnp.concatenate(sum_rows, axis=0)
    pl.semaphore_wait(barrier, owners - 1 + groups - 1)
    ctx[me_g] = jnp.zeros((2, padded), F32)
    ctx[me_g, 0:1, 0:params] = damp_ref[...]
    ctx[me_g, 1:2, 0:params] = rhs_ref[...]
    group_send(0, lambda peer: ctx.at[me_g], ctx.at[me_g])
    others = jnp.where(sub < count, other_col, 0).astype(F32).astype(BF16)
    other_out = dot(to_slot[owners:], others)
    send_terms(
        0, squares, jnp.where(last_lane < LANES // 2, other_out[:owners], other_out[owners:])
    )
    got, ids = get_message(0)
    group_col = iota((owners, LANES), 1).astype(F32)
    id_a = jnp.broadcast_to(ids[:, :1], (owners, LANES))
    id_b = jnp.broadcast_to(ids[:, LANES // 2 : LANES // 2 + 1], (owners, LANES))
    select = jnp.concatenate(
        [
            jnp.where(group_col == me_g.astype(F32), 1.0, 0.0),
            jnp.where(group_col == id_a, 1.0, 0.0),
            jnp.where(group_col == id_b, 1.0, 0.0),
        ],
        axis=0,
    )
    if 3 * owners < LANES:
        select_t = jnp.concatenate([select, jnp.zeros((LANES - 3 * owners, LANES), F32)], axis=0).T
    else:
        select_t = select.T
    select = select[:, :kpad].astype(BF16)
    select_t = select_t[:kpad, : 3 * owners].astype(BF16)

    def own_row(panel):
        return jnp.sum(jnp.where(wide_row == me_g, panel, 0.0), axis=0, keepdims=True)

    def split_row(value):
        spot = iota((1, LANES), 1)
        high = value.astype(BF16).astype(F32)
        middle = (value - high).astype(BF16).astype(F32)
        low = value - high - middle
        return (
            jnp.where(spot == 0, high, 0.0)
            + jnp.where(spot == 1, middle, 0.0)
            + jnp.where(spot == 2, low, 0.0)
        )

    def sum_over_groups(stage, got, scalar):
        panel = dot(select_t, got)[:groups]
        high = panel.astype(BF16).astype(F32)
        low = own_row(panel - high)
        parts = [low[:, c * LANES : (c + 1) * LANES] for c in range(tiles)]
        parts.append(jnp.zeros((1, LANES), F32) if scalar is None else split_row(scalar))
        parts.append(jnp.zeros((groups - tiles - 1, LANES), F32))
        extra = jnp.concatenate(parts, axis=0)
        head = high[:, : 3 * LANES]
        tail = jnp.concatenate([high[:, 3 * LANES :], extra], axis=1)
        wide[stage, me_g] = jnp.concatenate([head, tail], axis=0).astype(BF16)
        group_send(1 + stage, lambda peer: wide.at[stage, me_g], wide.at[stage, me_g])
        group_wait(wide.at[stage, pl.ds(0, groups - 1)], zrcv_sem, 1 + stage)
        out = jnp.zeros((groups, padded), F32)
        scalar_out = jnp.zeros((1, LANES), F32)
        for g in range(groups):
            part = wide[stage, g].astype(F32)
            out = out + jnp.concatenate([part[:groups], part[groups:, : 2 * LANES]], axis=1)
            extra = part[groups:, 2 * LANES :]
            low = jnp.concatenate([extra[c : c + 1] for c in range(tiles)], axis=1)
            out = out + jnp.where(wide_row == g, jnp.broadcast_to(low, out.shape), 0.0)
            scalar_out = scalar_out + extra[tiles : tiles + 1]
        return out, total(scalar_out)

    def send_panel(stage, panel, last):
        low = jnp.concatenate([panel, jnp.zeros((kpad - groups, padded), F32)], axis=0)
        out = dot(select, low.astype(BF16))
        put_message(stage, out[:owners], out[owners : 2 * owners], out[2 * owners :], last)

    def inputs_of(got):
        home = dot(from_home[:, :owners], got[:owners])
        far = dot(from_far[:, owners : 3 * owners], got[owners:])
        fill = jnp.zeros((kpad, width - padded), F32)
        home = jnp.concatenate([home, fill], axis=1)
        far = pltpu.roll(jnp.concatenate([far, fill], axis=1), params, 1)
        return (home + far).astype(BF16)

    summed, unused = sum_over_groups(0, got, None)
    group_wait(ctx.at[pl.ds(0, groups - 1)], zrcv_sem, 0)
    damping = jnp.concatenate([ctx[g, 0:1, :] for g in range(groups)], axis=0)
    right_side = jnp.concatenate([ctx[g, 1:2, :] for g in range(groups)], axis=0)
    diagonal = jnp.where(wide_lane < params, damping + summed, 1.0)
    direction = right_side / diagonal

    send_panel(
        1,
        direction,
        split(total(right_side * direction), 0)
        + split(total(damping * direction * direction), LANES // 2),
    )
    got, scalars = get_message(1)
    norm = total(jnp.where(last_lane < LANES // 2, scalars, 0.0))
    damped = total(jnp.where(last_lane < LANES // 2, 0.0, scalars))
    product = dot(inputs_of(got), jac[...], ((1,), (1,)))
    kept = product * keep
    projected = kept.astype(BF16)
    returned = dot(projected, jac[...])
    send_terms(2, returned, split(total(kept * projected.astype(F32)), 0))
    got, scalars = get_message(2)
    summed, square = sum_over_groups(1, got, total(scalars))
    step_size = norm / (damped + square)
    residual = right_side - step_size * (damping * direction + summed)
    scaled = residual / diagonal

    send_panel(3, scaled, split(total(residual * scaled), 0))
    got, scalars = get_message(3)
    next_norm = total(scalars)
    beta = next_norm / norm
    product = dot(inputs_of(got), jac[...], ((1,), (1,))) + beta * product
    kept = product * keep
    projected = kept.astype(BF16)
    returned = dot(projected, jac[...])
    first_direction = own_row(direction)
    own_damping = own_row(damping)
    next_direction = own_row(scaled) + beta * first_direction
    partial = total(kept * projected.astype(F32)) + total(
        own_damping * next_direction * next_direction
    )
    send_terms(4, returned, split(partial, 0))
    got, scalars = get_message(4)
    panel = dot(select_t, got)[:groups]
    panel = jnp.where(wide_lane == params, jnp.broadcast_to(total(scalars), panel.shape), panel)
    for g in range(groups):
        row_snd[g] = panel[g : g + 1]
    row_rcv[me_g] = own_row(panel)
    group_send(3, lambda peer: row_snd.at[peer], row_rcv.at[me_g])
    group_wait(row_rcv.at[pl.ds(0, groups - 1)], zrcv_sem, 3)
    out = row_rcv[0]
    for g in range(1, groups):
        out = out + row_rcv[g]
    one_lane = iota((1, padded), 1)
    curvature = total(jnp.where(one_lane == params, out, 0.0))
    next_step = next_norm / curvature
    image = own_damping * next_direction + out
    sol_ref[...] = (step_size * first_direction + next_step * next_direction)[:, :params]
    res_ref[...] = (own_row(residual) - next_step * image)[:, :params]

    for stage in range(5):
        block_wait(snd, snd_sem, stage)
    group_wait(ctx.at[pl.ds(0, groups - 1)], zsnd_sem, 0)
    for stage in range(2):
        group_wait(wide.at[stage, pl.ds(0, groups - 1)], zsnd_sem, 1 + stage)
    group_wait(row_snd.at[pl.ds(0, groups - 1)], zsnd_sem, 3)


def on_device(groups, owners, jacobians, destination, other_group, live_rows, damping, right_side):
    count, rows, width = jacobians.shape
    params = width // 2
    padded = (params + LANES - 1) // LANES * LANES
    vmem = pl.BlockSpec(memory_space=pltpu.VMEM)
    return pl.pallas_call(
        functools.partial(cg_kernel, groups, owners, count, rows, params),
        out_shape=(
            jax.ShapeDtypeStruct(right_side.shape, F32),
            jax.ShapeDtypeStruct(right_side.shape, F32),
        ),
        in_specs=[pl.BlockSpec(memory_space=pltpu.HBM)] * 6,
        out_specs=(vmem, vmem),
        scratch_shapes=[
            pltpu.VMEM((count * rows, width), BF16),
            pltpu.SMEM((count,), jnp.int32),
            pltpu.SMEM((count,), jnp.int32),
            pltpu.SMEM((count,), jnp.int32),
            pltpu.VMEM((1, params), F32),
            pltpu.VMEM((1, params), F32),
            pltpu.VMEM((owners * MSG, LANES), F32),
            pltpu.VMEM((owners * MSG, LANES), F32),
            pltpu.VMEM((5, owners * MSG, LANES), BF16),
            pltpu.VMEM((5, owners * MSG, LANES), BF16),
            pltpu.VMEM((groups, 2, padded), F32),
            pltpu.VMEM((2, groups, 2 * groups, 3 * LANES), BF16),
            pltpu.VMEM((groups, 1, padded), F32),
            pltpu.VMEM((groups, 1, padded), F32),
            pltpu.SemaphoreType.DMA((count,)),
            pltpu.SemaphoreType.DMA((5,)),
            pltpu.SemaphoreType.DMA((5,)),
            pltpu.SemaphoreType.DMA((5,)),
            pltpu.SemaphoreType.DMA((4,)),
            pltpu.SemaphoreType.DMA((4,)),
        ],
        compiler_params=pltpu.CompilerParams(
            collective_id=0, has_side_effects=True, vmem_limit_bytes=60 * 1024 * 1024
        ),
    )(
        jacobians.reshape(count * rows, width), destination, other_group, live_rows, damping, right_side
    )


def solution(mesh):
    placed = (
        P(("group", "block"), None, None),
        P(("group", "block")),
        P(("group", "block")),
        P(("group", "block")),
        P(("group", "block"), None),
        P(("group", "block"), None),
    )
    return jax.shard_map(
        functools.partial(on_device, mesh.shape["group"], mesh.shape["block"]),
        mesh=mesh,
        in_specs=placed,
        out_specs=(P(("group", "block"), None), P(("group", "block"), None)),
        check_vma=False,
    )
```

```python
import functools
import itertools

import jax
import jax.numpy as jnp
from jax import lax
from jax.experimental import pallas as pl
from jax.experimental.pallas import tpu as pltpu
from jax.sharding import PartitionSpec as P

LANES = 128
MSG = 16
F32 = jnp.float32
BF16 = jnp.bfloat16


def total(value):
    return jnp.sum(jnp.sum(value, axis=1, keepdims=True), axis=0, keepdims=True)


def iota(shape, dim):
    return lax.broadcasted_iota(jnp.int32, shape, dim)


def dot(left, right, contract=((1,), (0,))):
    return lax.dot_general(left, right, (contract, ((), ())), preferred_element_type=F32)


def block_dims(owners):
    return (4, 4, 2) if owners == 32 else (1, owners // 2, 2)


def distance(offset, dims):
    return sum(min(step, size - step) for step, size in zip(offset[:2], dims))


def peer_offsets(dims):
    offsets = list(itertools.product(*[range(size) for size in dims]))
    return sorted(offsets, key=lambda offset: (-distance(offset, dims), -offset[2]))


def opposite(offset, dims):
    return tuple((size - step) % size for step, size in zip(offset, dims))


def peer_at(me, offset, dims):
    x, y, core = me // (dims[1] * dims[2]), (me // dims[2]) % dims[1], me % dims[2]
    x, y, core = ((at + step) % size for at, step, size in zip((x, y, core), offset, dims))
    return (x * dims[1] + y) * dims[2] + core


def cg_kernel(
    groups, owners, count, rows, params,
    jac_hbm, dest_hbm, other_hbm, live_hbm, damp_hbm, rhs_hbm,
    out_ref,
    jac, dest_ref, other_ref, live_ref, damp_ref, rhs_ref,
    pack, unpack, snd, rcv, ctx, wide, row_snd, row_rcv,
    jac_sem, in_sem, snd_sem, rcv_sem, zsnd_sem, zrcv_sem,
):
    me_g = lax.axis_index("group")
    me_b = lax.axis_index("block")
    width = jac.shape[1]
    tiles = (params + LANES - 1) // LANES
    padded = tiles * LANES
    kpad = 16

    dims = block_dims(owners)
    offsets = peer_offsets(dims)
    peers = [peer_at(me_b, offset, dims) for offset in offsets]
    group_order = sorted(range(1, groups), key=lambda step: -min(step, groups - step))

    barrier = pltpu.get_barrier_semaphore()
    for peer in peers[:-1]:
        pl.semaphore_signal(
            barrier, inc=1, device_id=(me_g, peer), device_id_type=pl.DeviceIdType.MESH
        )
    for step in group_order:
        pl.semaphore_signal(
            barrier,
            inc=1,
            device_id=((me_g + step) % groups, me_b),
            device_id_type=pl.DeviceIdType.MESH,
        )

    def block_copy(k):
        part = pl.ds(k * rows, rows)
        return pltpu.make_async_copy(jac_hbm.at[part], jac.at[part], jac_sem.at[k])

    small = [
        pltpu.make_async_copy(source, target, in_sem.at[i])
        for i, (source, target) in enumerate(
            [
                (dest_hbm, dest_ref),
                (other_hbm, other_ref),
                (live_hbm, live_ref),
                (damp_hbm, damp_ref),
                (rhs_hbm, rhs_ref),
            ]
        )
    ]
    for copy in small:
        copy.start()
    for k in range(count):
        block_copy(k).start()

    def slot_part(slot):
        return pl.ds(slot * MSG, MSG)

    def block_send(stage):
        for slot, peer in enumerate(peers[:-1]):
            there = offsets.index(opposite(offsets[slot], dims))
            pltpu.make_async_remote_copy(
                src_ref=snd.at[stage, slot_part(slot)],
                dst_ref=rcv.at[stage, slot_part(there)],
                send_sem=snd_sem.at[stage],
                recv_sem=rcv_sem.at[stage],
                device_id=(me_g, peer),
                device_id_type=pl.DeviceIdType.MESH,
            ).start()
        rcv[stage, slot_part(owners - 1)] = snd[stage, slot_part(owners - 1)]

    def block_wait(ref, sem, stage):
        part = ref.at[stage, pl.ds(0, (owners - 1) * MSG)]
        pltpu.make_async_copy(part, part, sem.at[stage]).wait()

    def group_send(stage, src_of, dst):
        for step in group_order:
            peer = (me_g + step) % groups
            pltpu.make_async_remote_copy(
                src_ref=src_of(peer),
                dst_ref=dst,
                send_sem=zsnd_sem.at[stage],
                recv_sem=zrcv_sem.at[stage],
                device_id=(peer, me_b),
                device_id_type=pl.DeviceIdType.MESH,
            ).start()

    def group_wait(part, sem, stage):
        pltpu.make_async_copy(part, part, sem.at[stage]).wait()

    for copy in small:
        copy.wait()

    sub = iota((kpad, LANES), 0)
    lane = iota((kpad, LANES), 1)
    dest_col = jnp.full((kpad, LANES), -1, jnp.int32)
    dest_row = jnp.full((kpad, LANES), -1, jnp.int32)
    live_col = jnp.zeros((kpad, LANES), jnp.int32)
    other_col = jnp.zeros((kpad, LANES), jnp.int32)
    for k in range(count):
        dest_col = jnp.where(sub == k, dest_ref[k], dest_col)
        dest_row = jnp.where(lane == k, dest_ref[k], dest_row)
        live_col = jnp.where(sub == k, live_ref[k], live_col)
        other_col = jnp.where(sub == k, other_ref[k], other_col)
    same = jnp.where((dest_col == dest_row) & (dest_row >= 0), 1.0, 0.0)
    rank_row = jnp.sum(jnp.where(sub < lane, same, 0.0), axis=0, keepdims=True)
    rank_col = jnp.sum(jnp.where(lane < sub, same, 0.0), axis=1, keepdims=True)
    slot = iota((3 * owners, LANES), 0)
    dest_rows = jnp.broadcast_to(dest_row[:1], (3 * owners, LANES))
    rank_rows = jnp.broadcast_to(rank_row, (3 * owners, LANES))
    slot_peer = iota((owners, LANES), 0)
    for number, peer in enumerate(peers):
        slot_peer = jnp.where(iota((owners, LANES), 0) == number, peer, slot_peer)
    slot_hit = dest_rows == jnp.concatenate([slot_peer] * 3, axis=0)
    slot_rank = (slot // owners - 1).astype(F32)
    to_slot = jnp.where(slot_hit & ((slot < owners) | (rank_rows == slot_rank)), 1.0, 0.0)
    to_slot = to_slot[:, :kpad].astype(BF16)
    slot_lane = iota((kpad, LANES), 1)
    lane_peer = jnp.zeros((kpad, LANES), jnp.int32)
    for number, peer in enumerate(peers):
        lane_peer = jnp.where(slot_lane % owners == number, peer, lane_peer)
    lane_hit = dest_col == lane_peer
    lane_rank = (slot_lane // owners - 1).astype(F32)
    rank_cols = jnp.broadcast_to(rank_col, (kpad, LANES))
    from_home = jnp.where(lane_hit & (slot_lane < owners), 1.0, 0.0).astype(BF16)
    from_far = jnp.where(
        lane_hit & (slot_lane >= owners) & (rank_cols == lane_rank), 1.0, 0.0
    ).astype(BF16)
    keep = jnp.concatenate(
        [jnp.where((sub == k) & (lane < live_col), 1.0, 0.0) for k in range(count)], axis=1
    )
    panel_lane = iota((kpad, padded), 1)

    def put_rows(first, value):
        for c in range(tiles):
            pack[pl.ds(first + c, owners, stride=MSG), :] = value[:, c * LANES : (c + 1) * LANES]

    def put_message(stage, home, far_a, far_b, last):
        put_rows(0, home)
        put_rows(tiles, far_a)
        put_rows(2 * tiles, far_b)
        pack[pl.ds(3 * tiles, owners, stride=MSG), :] = last
        snd[stage] = pack[...].astype(BF16)
        block_send(stage)

    def send_terms(stage, terms, last):
        home = jnp.where(panel_lane < params, terms[:, :padded], 0.0)
        far = jnp.where(panel_lane < params, pltpu.roll(terms, params, 1)[:, :padded], 0.0)
        high = home.astype(BF16)
        low = (home - high.astype(F32)).astype(BF16)
        home_out = dot(to_slot[:owners], high) + dot(to_slot[:owners], low)
        far_out = dot(to_slot[owners:], far.astype(BF16))
        put_message(stage, home_out, far_out[:owners], far_out[owners:], last)

    def get_message(stage):
        block_wait(rcv, rcv_sem, stage)
        unpack[...] = rcv[stage].astype(F32)

        def row(c):
            return unpack[pl.ds(c, owners, stride=MSG), :]

        parts = [
            jnp.concatenate([row(s * tiles + c) for c in range(tiles)], axis=1) for s in range(3)
        ]
        return jnp.concatenate(parts, axis=0).astype(BF16), row(3 * tiles)

    last_lane = iota((owners, LANES), 1)

    def split(value, first):
        high = value.astype(BF16).astype(F32)
        middle = (value - high).astype(BF16).astype(F32)
        low = value - high - middle
        out = jnp.where(last_lane == first, jnp.broadcast_to(high, last_lane.shape), 0.0)
        out = out + jnp.where(last_lane == first + 1, jnp.broadcast_to(middle, last_lane.shape), 0.0)
        return out + jnp.where(last_lane == first + 2, jnp.broadcast_to(low, last_lane.shape), 0.0)

    wide_lane = iota((groups, padded), 1)
    wide_row = iota((groups, padded), 0)
    sum_rows = []
    for k in range(count):
        block_copy(k).wait()
        block = jac[k * rows : (k + 1) * rows, :].astype(F32)
        live = iota((rows, width), 0) < live_ref[k]
        kept = jnp.where(live, block, 0.0)
        sum_rows.append(jnp.sum(kept * kept, axis=0, keepdims=True))
    sum_rows += [jnp.zeros((1, width), F32)] * (kpad - count)
    squares = jnp.concatenate(sum_rows, axis=0)
    pl.semaphore_wait(barrier, owners - 1 + groups - 1)
    ctx[me_g] = jnp.zeros((2, padded), F32)
    ctx[me_g, 0:1, 0:params] = damp_ref[...]
    ctx[me_g, 1:2, 0:params] = rhs_ref[...]
    group_send(0, lambda peer: ctx.at[me_g], ctx.at[me_g])
    others = jnp.where(sub < count, other_col, 0).astype(F32).astype(BF16)
    other_out = dot(to_slot[owners:], others)
    send_terms(
        0, squares, jnp.where(last_lane < LANES // 2, other_out[:owners], other_out[owners:])
    )
    got, ids = get_message(0)
    group_col = iota((owners, LANES), 1).astype(F32)
    id_a = jnp.broadcast_to(ids[:, :1], (owners, LANES))
    id_b = jnp.broadcast_to(ids[:, LANES // 2 : LANES // 2 + 1], (owners, LANES))
    select = jnp.concatenate(
        [
            jnp.where(group_col == me_g.astype(F32), 1.0, 0.0),
            jnp.where(group_col == id_a, 1.0, 0.0),
            jnp.where(group_col == id_b, 1.0, 0.0),
        ],
        axis=0,
    )
    if 3 * owners < LANES:
        select_t = jnp.concatenate([select, jnp.zeros((LANES - 3 * owners, LANES), F32)], axis=0).T
    else:
        select_t = select.T
    select = select[:, :kpad].astype(BF16)
    select_t = select_t[:kpad, : 3 * owners].astype(BF16)

    def own_row(panel):
        return jnp.sum(jnp.where(wide_row == me_g, panel, 0.0), axis=0, keepdims=True)

    def split_row(value):
        spot = iota((1, LANES), 1)
        high = value.astype(BF16).astype(F32)
        middle = (value - high).astype(BF16).astype(F32)
        low = value - high - middle
        return (
            jnp.where(spot == 0, high, 0.0)
            + jnp.where(spot == 1, middle, 0.0)
            + jnp.where(spot == 2, low, 0.0)
        )

    def sum_over_groups(stage, got, scalar):
        panel = dot(select_t, got)[:groups]
        high = panel.astype(BF16).astype(F32)
        low = own_row(panel - high)
        parts = [low[:, c * LANES : (c + 1) * LANES] for c in range(tiles)]
        parts.append(jnp.zeros((1, LANES), F32) if scalar is None else split_row(scalar))
        parts.append(jnp.zeros((groups - tiles - 1, LANES), F32))
        extra = jnp.concatenate(parts, axis=0)
        head = high[:, : 3 * LANES]
        tail = jnp.concatenate([high[:, 3 * LANES :], extra], axis=1)
        wide[stage, me_g] = jnp.concatenate([head, tail], axis=0).astype(BF16)
        group_send(1 + stage, lambda peer: wide.at[stage, me_g], wide.at[stage, me_g])
        group_wait(wide.at[stage, pl.ds(0, groups - 1)], zrcv_sem, 1 + stage)
        out = jnp.zeros((groups, padded), F32)
        scalar_out = jnp.zeros((1, LANES), F32)
        for g in range(groups):
            part = wide[stage, g].astype(F32)
            out = out + jnp.concatenate([part[:groups], part[groups:, : 2 * LANES]], axis=1)
            extra = part[groups:, 2 * LANES :]
            low = jnp.concatenate([extra[c : c + 1] for c in range(tiles)], axis=1)
            out = out + jnp.where(wide_row == g, jnp.broadcast_to(low, out.shape), 0.0)
            scalar_out = scalar_out + extra[tiles : tiles + 1]
        return out, total(scalar_out)

    def send_panel(stage, panel, last):
        low = jnp.concatenate([panel, jnp.zeros((kpad - groups, padded), F32)], axis=0)
        out = dot(select, low.astype(BF16))
        put_message(stage, out[:owners], out[owners : 2 * owners], out[2 * owners :], last)

    def inputs_of(got):
        home = dot(from_home[:, :owners], got[:owners])
        far = dot(from_far[:, owners : 3 * owners], got[owners:])
        fill = jnp.zeros((kpad, width - padded), F32)
        home = jnp.concatenate([home, fill], axis=1)
        far = pltpu.roll(jnp.concatenate([far, fill], axis=1), params, 1)
        return (home + far).astype(BF16)

    summed, unused = sum_over_groups(0, got, None)
    group_wait(ctx.at[pl.ds(0, groups - 1)], zrcv_sem, 0)
    damping = jnp.concatenate([ctx[g, 0:1, :] for g in range(groups)], axis=0)
    right_side = jnp.concatenate([ctx[g, 1:2, :] for g in range(groups)], axis=0)
    diagonal = jnp.where(wide_lane < params, damping + summed, 1.0)
    direction = right_side / diagonal

    send_panel(
        1,
        direction,
        split(total(right_side * direction), 0)
        + split(total(damping * direction * direction), LANES // 2),
    )
    got, scalars = get_message(1)
    norm = total(jnp.where(last_lane < LANES // 2, scalars, 0.0))
    damped = total(jnp.where(last_lane < LANES // 2, 0.0, scalars))
    product = dot(inputs_of(got), jac[...], ((1,), (1,)))
    kept = product * keep
    projected = kept.astype(BF16)
    returned = dot(projected, jac[...])
    send_terms(2, returned, split(total(kept * projected.astype(F32)), 0))
    got, scalars = get_message(2)
    summed, square = sum_over_groups(1, got, total(scalars))
    step_size = norm / (damped + square)
    residual = right_side - step_size * (damping * direction + summed)
    scaled = residual / diagonal

    send_panel(3, scaled, split(total(residual * scaled), 0))
    got, scalars = get_message(3)
    next_norm = total(scalars)
    beta = next_norm / norm
    product = dot(inputs_of(got), jac[...], ((1,), (1,))) + beta * product
    kept = product * keep
    projected = kept.astype(BF16)
    returned = dot(projected, jac[...])
    first_direction = own_row(direction)
    own_damping = own_row(damping)
    next_direction = own_row(scaled) + beta * first_direction
    partial = total(kept * projected.astype(F32)) + total(
        own_damping * next_direction * next_direction
    )
    send_terms(4, returned, split(partial, 0))
    got, scalars = get_message(4)
    panel = dot(select_t, got)[:groups]
    panel = jnp.where(wide_lane == params, jnp.broadcast_to(total(scalars), panel.shape), panel)
    for g in range(groups):
        row_snd[g] = panel[g : g + 1]
    row_rcv[me_g] = own_row(panel)
    group_send(3, lambda peer: row_snd.at[peer], row_rcv.at[me_g])
    group_wait(row_rcv.at[pl.ds(0, groups - 1)], zrcv_sem, 3)
    out = row_rcv[0]
    for g in range(1, groups):
        out = out + row_rcv[g]
    one_lane = iota((1, padded), 1)
    curvature = total(jnp.where(one_lane == params, out, 0.0))
    next_step = next_norm / curvature
    image = own_damping * next_direction + out
    out_ref[0:1] = (step_size * first_direction + next_step * next_direction)[:, :params]
    out_ref[1:2] = (own_row(residual) - next_step * image)[:, :params]

    for stage in range(5):
        block_wait(snd, snd_sem, stage)
    group_wait(ctx.at[pl.ds(0, groups - 1)], zsnd_sem, 0)
    for stage in range(2):
        group_wait(wide.at[stage, pl.ds(0, groups - 1)], zsnd_sem, 1 + stage)
    group_wait(row_snd.at[pl.ds(0, groups - 1)], zsnd_sem, 3)


def on_device(groups, owners, jacobians, destination, other_group, live_rows, damping, right_side):
    count, rows, width = jacobians.shape
    params = width // 2
    padded = (params + LANES - 1) // LANES * LANES
    vmem = pl.BlockSpec(memory_space=pltpu.VMEM)
    out = pl.pallas_call(
        functools.partial(cg_kernel, groups, owners, count, rows, params),
        out_shape=(
            jax.ShapeDtypeStruct((2, params), F32),
        ),
        in_specs=[pl.BlockSpec(memory_space=pltpu.HBM)] * 6,
        out_specs=(vmem,),
        scratch_shapes=[
            pltpu.VMEM((count * rows, width), BF16),
            pltpu.SMEM((count,), jnp.int32),
            pltpu.SMEM((count,), jnp.int32),
            pltpu.SMEM((count,), jnp.int32),
            pltpu.VMEM((1, params), F32),
            pltpu.VMEM((1, params), F32),
            pltpu.VMEM((owners * MSG, LANES), F32),
            pltpu.VMEM((owners * MSG, LANES), F32),
            pltpu.VMEM((5, owners * MSG, LANES), BF16),
            pltpu.VMEM((5, owners * MSG, LANES), BF16),
            pltpu.VMEM((groups, 2, padded), F32),
            pltpu.VMEM((2, groups, 2 * groups, 3 * LANES), BF16),
            pltpu.VMEM((groups, 1, padded), F32),
            pltpu.VMEM((groups, 1, padded), F32),
            pltpu.SemaphoreType.DMA((count,)),
            pltpu.SemaphoreType.DMA((5,)),
            pltpu.SemaphoreType.DMA((5,)),
            pltpu.SemaphoreType.DMA((5,)),
            pltpu.SemaphoreType.DMA((4,)),
            pltpu.SemaphoreType.DMA((4,)),
        ],
        compiler_params=pltpu.CompilerParams(
            collective_id=0, has_side_effects=True, vmem_limit_bytes=60 * 1024 * 1024
        ),
    )(
        jacobians.reshape(count * rows, width), destination, other_group, live_rows, damping, right_side
    )[0]
    return out[0:1], out[1:2]


def solution(mesh):
    placed = (
        P(("group", "block"), None, None),
        P(("group", "block")),
        P(("group", "block")),
        P(("group", "block")),
        P(("group", "block"), None),
        P(("group", "block"), None),
    )
    return jax.shard_map(
        functools.partial(on_device, mesh.shape["group"], mesh.shape["block"]),
        mesh=mesh,
        in_specs=placed,
        out_specs=(P(("group", "block"), None), P(("group", "block"), None)),
        check_vma=False,
    )
```

```python
import functools
import itertools

import jax
import jax.numpy as jnp
from jax import lax
from jax.experimental import pallas as pl
from jax.experimental.pallas import tpu as pltpu
from jax.sharding import PartitionSpec as P

LANES = 128
MSG = 16
TERMS = 256
PANEL = 96
F32 = jnp.float32
BF16 = jnp.bfloat16


def total(value):
    return jnp.sum(jnp.sum(value, axis=1, keepdims=True), axis=0, keepdims=True)


def iota(shape, dim):
    return lax.broadcasted_iota(jnp.int32, shape, dim)


def dot(left, right, contract=((1,), (0,))):
    return lax.dot_general(left, right, (contract, ((), ())), preferred_element_type=F32)


def block_dims(owners):
    return (4, 4, 2) if owners == 32 else (1, owners // 2, 2)


def distance(offset, dims):
    return sum(min(step, size - step) for step, size in zip(offset[:2], dims))


def peer_offsets(dims):
    offsets = list(itertools.product(*[range(size) for size in dims]))
    return sorted(offsets, key=lambda offset: (-distance(offset, dims), -offset[2]))


def opposite(offset, dims):
    return tuple((size - step) % size for step, size in zip(offset, dims))


def peer_at(me, offset, dims):
    x, y, core = me // (dims[1] * dims[2]), (me // dims[2]) % dims[1], me % dims[2]
    x, y, core = ((at + step) % size for at, step, size in zip((x, y, core), offset, dims))
    return (x * dims[1] + y) * dims[2] + core


def scalar_row(last, total_rows):
    spot = (iota((16, total_rows), 1) & (MSG - 1)) == last
    return jnp.where(spot & (iota((16, total_rows), 0) == 0), 1.0, 0.0).astype(BF16)


def cg_kernel(
    groups, owners, count, rows, params,
    jac_hbm, dest_hbm, other_hbm, live_hbm, damp_hbm, rhs_hbm,
    out_ref,
    jac, jac_t, dest_ref, other_ref, live_ref, damp_ref, rhs_ref,
    unpack, extras, term_map, input_map, panel_map, row_map, snd, rcv, ctx, wide, row_snd, row_rcv,
    jac_sem, in_sem, snd_sem, rcv_sem, zsnd_sem, zrcv_sem,
):
    me_g = lax.axis_index("group")
    me_b = lax.axis_index("block")
    width = jac.shape[1]
    tiles = (params + LANES - 1) // LANES
    padded = tiles * LANES
    kpad = 16
    raw = width // LANES
    total_rows = owners * MSG
    late = min(8, owners // 2)
    chunks = sorted({(0, late), (late, 2 * late), (2 * late, owners)} - {(owners, owners)})

    dims = block_dims(owners)
    offsets = peer_offsets(dims)
    peers = [peer_at(me_b, offset, dims) for offset in offsets]
    group_order = sorted(range(1, groups), key=lambda step: -min(step, groups - step))

    barrier = pltpu.get_barrier_semaphore()
    for step in group_order:
        pl.semaphore_signal(
            barrier,
            inc=1,
            device_id=((me_g + step) % groups, me_b),
            device_id_type=pl.DeviceIdType.MESH,
        )
    for peer in peers[:-1]:
        pl.semaphore_signal(
            barrier, inc=1, device_id=(me_g, peer), device_id_type=pl.DeviceIdType.MESH
        )

    def block_copy(k):
        part = pl.ds(k * rows, rows)
        return pltpu.make_async_copy(jac_hbm.at[part], jac.at[part], jac_sem.at[k])

    small = [
        pltpu.make_async_copy(source, target, in_sem.at[i])
        for i, (source, target) in enumerate(
            [
                (dest_hbm, dest_ref),
                (other_hbm, other_ref),
                (live_hbm, live_ref),
                (damp_hbm, damp_ref),
                (rhs_hbm, rhs_ref),
            ]
        )
    ]
    for copy in small:
        copy.start()
    for k in range(count):
        block_copy(k).start()

    def slot_part(slot):
        return pl.ds(slot * MSG, MSG)

    def block_send(stage, first, end):
        for slot in range(first, min(end, owners - 1)):
            there = offsets.index(opposite(offsets[slot], dims))
            pltpu.make_async_remote_copy(
                src_ref=snd.at[stage, slot_part(slot)],
                dst_ref=rcv.at[stage, slot_part(there)],
                send_sem=snd_sem.at[stage],
                recv_sem=rcv_sem.at[stage, 0 if there < late else 1],
                device_id=(me_g, peers[slot]),
                device_id_type=pl.DeviceIdType.MESH,
            ).start()

    def block_wait_near(stage):
        part = rcv.at[stage, pl.ds(late * MSG, (owners - 1 - late) * MSG)]
        pltpu.make_async_copy(part, part, rcv_sem.at[stage, 1]).wait()

    def block_wait_far(stage):
        part = rcv.at[stage, pl.ds(0, late * MSG)]
        pltpu.make_async_copy(part, part, rcv_sem.at[stage, 0]).wait()

    def block_wait_sent(stage):
        part = snd.at[stage, pl.ds(0, (owners - 1) * MSG)]
        pltpu.make_async_copy(part, part, snd_sem.at[stage]).wait()

    def group_send(stage, src_of, dst):
        for step in group_order:
            peer = (me_g + step) % groups
            pltpu.make_async_remote_copy(
                src_ref=src_of(peer),
                dst_ref=dst,
                send_sem=zsnd_sem.at[stage],
                recv_sem=zrcv_sem.at[stage],
                device_id=(peer, me_b),
                device_id_type=pl.DeviceIdType.MESH,
            ).start()

    def group_wait(part, sem, stage):
        pltpu.make_async_copy(part, part, sem.at[stage]).wait()

    for copy in small:
        copy.wait()

    half = params // LANES
    near = groups * tiles
    sub = iota((kpad, TERMS), 0)
    lane = iota((kpad, TERMS), 1)
    block_lane = lane & (kpad - 1)
    dest_col = jnp.full((kpad, TERMS), -1, jnp.int32)
    dest_row = jnp.full((kpad, TERMS), -1, jnp.int32)
    live_col = jnp.zeros((kpad, LANES), jnp.int32)
    other_col = jnp.zeros((kpad, LANES), jnp.int32)
    for k in range(count):
        dest_col = jnp.where(sub == k, dest_ref[k], dest_col)
        dest_row = jnp.where(block_lane == k, dest_ref[k], dest_row)
        live_col = jnp.where(sub[:, :LANES] == k, live_ref[k], live_col)
        other_col = jnp.where(sub[:, :LANES] == k, other_ref[k], other_col)
    same = jnp.where((dest_col == dest_row) & (dest_row >= 0), 1.0, 0.0)
    rank_row = jnp.sum(jnp.where(sub < block_lane, same, 0.0), axis=0, keepdims=True)
    rank_col = jnp.sum(jnp.where((lane < sub), same, 0.0), axis=1, keepdims=True)
    slot_peer = jnp.zeros((owners, TERMS), jnp.int32)
    for number, peer in enumerate(peers):
        slot_peer = jnp.where(iota((owners, TERMS), 0) == number, peer, slot_peer)
    hit = jnp.where(jnp.broadcast_to(dest_row[:1], (owners, TERMS)) == slot_peer, 1.0, 0.0)
    rank = jnp.broadcast_to(rank_row, (owners, TERMS))
    to_slot = jnp.concatenate(
        [hit, jnp.where(rank == 0.0, hit, 0.0), jnp.where(rank == 1.0, hit, 0.0)], axis=0
    ).astype(BF16)

    def segment(row):
        return jnp.where(row < tiles, 0, jnp.where(row < 2 * tiles, 1, jnp.where(row < 3 * tiles, 2, 0)))

    row_at = iota((total_rows, 3 * owners), 0)
    slot_at = iota((total_rows, 3 * owners), 1)
    spread = (
        jnp.where(
            (row_at >> 4) + owners * segment(row_at & (MSG - 1)) == slot_at, 1.0, 0.0
        )
    ).astype(BF16)
    row = iota((total_rows, TERMS), 0) & (MSG - 1)
    term_lane = iota((total_rows, TERMS), 1)
    tile = term_lane >> 4
    last = 3 * tiles
    wanted = jnp.where(row < tiles, row, jnp.where(row < 2 * tiles, row - tiles, row - 2 * tiles) + half)
    allowed = (row < last) & ((tile == wanted) | ((row < tiles) & (tile == raw + row)))
    terms_to_rows = jnp.where(allowed, dot(spread, to_slot), 0.0)
    terms_to_rows = jnp.where((row == last) & (term_lane == kpad - 1), 1.0, terms_to_rows)
    term_map[...] = terms_to_rows.astype(BF16)
    input_map[...] = terms_to_rows.T[: raw * kpad].astype(BF16)
    keep = jnp.concatenate(
        [
            jnp.where((sub[:, :LANES] == k) & (lane[:, :LANES] < live_col), 1.0, 0.0)
            for k in range(count)
        ],
        axis=1,
    )
    def panel_target(row, ids_a, ids_b):
        part = segment(row)
        far = jnp.where(part == 1, row - tiles, row - 2 * tiles) * groups + near
        far = far.astype(F32) + jnp.where(part == 1, ids_a, ids_b)
        home = (row * groups + me_g).astype(F32)
        return jnp.where(row == last, float(2 * near), jnp.where(row < tiles, home, far))

    others = other_col.astype(F32).astype(BF16)
    ids = dot(to_slot[owners:, :kpad], others)
    there = jnp.zeros((owners, LANES), jnp.int32)
    for number, offset in enumerate(offsets):
        place = offsets.index(opposite(offset, dims))
        there = jnp.where(iota((owners, LANES), 0) == number, place, there)
    slot_lane = iota((owners, LANES), 1)
    targets = panel_target(slot_lane & (MSG - 1), ids[:owners], ids[owners:])
    per_tile = LANES // MSG
    unpack[...] = jnp.zeros((total_rows, LANES), F32)
    unpack[pl.ds(last, owners, stride=MSG), :] = jnp.where(
        (slot_lane >> 4) == (there & (per_tile - 1)), targets, 0.0
    )

    def tiles_of(value, first, number):
        return [value[:, c * LANES : (c + 1) * LANES] for c in range(first, first + number)]

    def send_rows(stage, row_of, values, extra=None):
        for first, end in chunks:
            part = pl.ds(first * MSG, (end - first) * MSG)
            out = dot(row_of[part], values)
            out = (out if extra is None else out + extra[part]).astype(BF16)
            snd[stage, part] = out
            block_send(stage, first, end)
        rcv[stage, slot_part(owners - 1)] = out[-MSG:]

    def receive_rows(stage, map_ref):
        block_wait_near(stage)
        near_rows = pl.ds(late * MSG, total_rows - late * MSG)
        out = dot(map_ref[:, late * MSG :], rcv[stage, near_rows])
        block_wait_far(stage)
        return out + dot(map_ref[:, : late * MSG], rcv[stage, pl.ds(0, late * MSG)])

    def send_terms(stage, terms, last_row, extra=None):
        high = terms.astype(BF16)
        low = (terms[:, :padded] - high[:, :padded].astype(F32)).astype(BF16)
        parts = tiles_of(high, 0, raw)
        if last_row is not None:
            carrier = jnp.where(sub[:, :LANES] == kpad - 1, last_row, terms[:, :LANES])
            parts[0] = carrier.astype(BF16)
        parts += tiles_of(low, 0, tiles)
        blank = jnp.zeros((kpad, LANES), BF16)
        parts += [blank] * (TERMS // kpad - len(parts))
        send_rows(stage, term_map, jnp.concatenate(parts, axis=0), extra)

    wide_lane = iota((groups, padded), 1)
    wide_row = iota((groups, padded), 0)
    valid = wide_lane < params
    shift = params % LANES

    def receive_terms(stage):
        if stage == 0:
            out = dot(panel_map[...], rcv[0])
        else:
            out = receive_rows(stage, panel_map)
        home = jnp.concatenate([out[c * groups : (c + 1) * groups] for c in range(tiles)], axis=1)
        far = jnp.concatenate(
            [out[near + c * groups : near + (c + 1) * groups] for c in range(tiles)], axis=1
        )
        panel = home + pltpu.roll(far, padded - shift, 1)
        return jnp.where(valid, panel, 0.0), out[2 * near : 2 * near + 1]

    def send_panel(stage, panel, last_row):
        parts = tiles_of(panel, 0, tiles) + tiles_of(pltpu.roll(panel, shift, 1), 0, tiles)
        parts.append(jnp.broadcast_to(last_row, (groups, LANES)))
        parts.append(jnp.zeros((PANEL - 2 * near - groups, LANES), F32))
        send_rows(stage, row_map, jnp.concatenate(parts, axis=0).astype(BF16))

    def receive_inputs(stage):
        out = receive_rows(stage, input_map)
        inputs = jnp.concatenate([out[t * kpad : (t + 1) * kpad] for t in range(raw)], axis=1)
        return inputs.astype(BF16)

    one = iota((1, LANES), 1)

    def split(value, first):
        high = value.astype(BF16).astype(F32)
        middle = (value - high).astype(BF16).astype(F32)
        low = value - high - middle
        out = jnp.where(one == first, high, 0.0) + jnp.where(one == first + 1, middle, 0.0)
        return out + jnp.where(one == first + 2, low, 0.0)

    def lanes_of(value):
        value = jnp.sum(value, axis=0, keepdims=True)
        folded = sum(tiles_of(value, 0, tiles)[1:], value[:, :LANES])
        folded = folded + pltpu.roll(folded, LANES // 2, 1)
        high = folded.astype(BF16).astype(F32)
        return jnp.where(one < LANES // 2, high, folded - high)

    def own_row(panel):
        return jnp.sum(jnp.where(wide_row == me_g, panel, 0.0), axis=0, keepdims=True)

    def sum_over_groups(stage, panel, scalar):
        high = panel.astype(BF16).astype(F32)
        low = own_row(panel - high)
        parts = tiles_of(low, 0, tiles)
        scalar = jnp.zeros((1, LANES), F32) if scalar is None else scalar
        first = scalar.astype(BF16).astype(F32)
        second = (scalar - first).astype(BF16).astype(F32)
        parts += [first, second, scalar - first - second]
        extra = jnp.concatenate(parts, axis=0)
        head = high[:, : 3 * LANES]
        tail = jnp.concatenate([high[:, 3 * LANES :], extra], axis=1)
        wide[stage, me_g] = jnp.concatenate([head, tail], axis=0).astype(BF16)
        group_send(1 + stage, lambda peer: wide.at[stage, me_g], wide.at[stage, me_g])

    def summed_groups(stage):
        group_wait(wide.at[stage, pl.ds(0, groups - 1)], zrcv_sem, 1 + stage)
        out = jnp.zeros((groups, padded), F32)
        for g in range(groups):
            part = wide[stage, g].astype(F32)
            out = out + jnp.concatenate([part[:groups], part[groups:, : 2 * LANES]], axis=1)
            extras[stage, g * groups : (g + 1) * groups] = part[groups:, 2 * LANES :]
        rest = [extras[stage, pl.ds(c, groups, stride=groups), :] for c in range(groups)]
        scalar = total(rest[tiles] + rest[tiles + 1] + rest[tiles + 2])
        return out + jnp.concatenate(rest[:tiles], axis=1), scalar

    sum_rows = []
    for k in range(count):
        block_copy(k).wait()
        block = jac[k * rows : (k + 1) * rows, :].astype(F32)
        live = iota((rows, width), 0) < live_ref[k]
        kept = jnp.where(live, block, 0.0)
        sum_rows.append(jnp.sum(kept * kept, axis=0, keepdims=True))
        jac_t[:, k * rows : (k + 1) * rows] = jac[k * rows : (k + 1) * rows, :].T
    sum_rows += [jnp.zeros((1, width), F32)] * (kpad - count)
    squares = jnp.concatenate(sum_rows, axis=0)

    ctx[me_g] = jnp.zeros((2, padded), F32)
    ctx[me_g, 0:1, 0:params] = damp_ref[...]
    ctx[me_g, 1:2, 0:params] = rhs_ref[...]
    pl.semaphore_wait(barrier, owners - 1 + groups - 1)
    send_terms(0, squares, None, unpack)
    group_send(0, lambda peer: ctx.at[me_g], ctx.at[me_g])
    block_wait_near(0)
    block_wait_far(0)
    decode_lane = iota((kpad, total_rows), 1)
    decode = jnp.where(
        ((decode_lane & (MSG - 1)) == last)
        & ((decode_lane >> 4) // per_tile == iota((kpad, total_rows), 0)),
        1.0,
        0.0,
    ).astype(BF16)
    decoded = dot(decode, rcv[0])
    target = jnp.concatenate(
        [
            jnp.broadcast_to(decoded[t : t + 1], (groups, LANES))
            for t in range((total_rows + LANES - 1) // LANES)
        ],
        axis=1,
    )[:, :total_rows]
    panel_row = iota((groups, total_rows), 0).astype(F32)
    rows_to_panel = jnp.concatenate(
        [
            jnp.where(target == panel_row + float(first), 1.0, 0.0)
            for first in range(0, LANES, groups)
        ],
        axis=0,
    )
    panel_map[...] = rows_to_panel[:PANEL].astype(BF16)
    panel, unused = receive_terms(0)
    sum_over_groups(0, panel, None)
    row_map[...] = rows_to_panel.T[:, :PANEL].astype(BF16)
    group_wait(ctx.at[pl.ds(0, groups - 1)], zrcv_sem, 0)
    damping = jnp.concatenate([ctx[g, 0:1, :] for g in range(groups)], axis=0)
    right_side = jnp.concatenate([ctx[g, 1:2, :] for g in range(groups)], axis=0)
    summed, unused = summed_groups(0)
    diagonal = jnp.where(valid, damping + summed, 1.0)
    direction = right_side / diagonal

    send_panel(1, direction, lanes_of(right_side * direction))
    first_direction = own_row(direction)
    own_damping = own_row(damping)
    damped_direction = damping * direction
    damped = total(own_damping * first_direction * first_direction)
    inputs = receive_inputs(1)
    product = dot(inputs, jac_t[...])
    kept = product * keep
    projected = kept.astype(BF16)
    returned = dot(projected, jac[...])
    send_terms(2, returned, split(damped + total(kept * projected.astype(F32)), 0))
    scalars = dot(scalar_row(last, total_rows), rcv[1])[:1]
    norm = total(scalars)
    panel, scalars = receive_terms(2)
    sum_over_groups(1, panel, scalars)
    summed, curvature = summed_groups(1)
    step_size = norm / curvature
    residual = right_side - step_size * (damped_direction + summed)
    scaled = residual / diagonal

    send_panel(3, scaled, lanes_of(residual * scaled))
    own_scaled = own_row(scaled)
    own_residual = own_row(residual)
    inputs = receive_inputs(3)
    next_norm = total(dot(scalar_row(last, total_rows), rcv[3])[:1])
    beta = next_norm / norm
    product = dot(inputs, jac_t[...]) + beta * product
    kept = product * keep
    projected = kept.astype(BF16)
    returned = dot(projected, jac[...])
    next_direction = own_scaled + beta * first_direction
    partial = total(kept * projected.astype(F32)) + total(
        own_damping * next_direction * next_direction
    )
    send_terms(4, returned, split(partial, 0))
    panel, scalars = receive_terms(4)
    panel = jnp.where(wide_lane == params, jnp.broadcast_to(total(scalars), panel.shape), panel)
    for g in range(groups):
        row_snd[g] = panel[g : g + 1]
    row_rcv[me_g] = own_row(panel)
    group_send(3, lambda peer: row_snd.at[peer], row_rcv.at[me_g])
    group_wait(row_rcv.at[pl.ds(0, groups - 1)], zrcv_sem, 3)
    out = row_rcv[0]
    for g in range(1, groups):
        out = out + row_rcv[g]
    one_lane = iota((1, padded), 1)
    curvature = total(jnp.where(one_lane == params, out, 0.0))
    next_step = next_norm / curvature
    image = own_damping * next_direction + out
    out_ref[0:1] = (step_size * first_direction + next_step * next_direction)[:, :params]
    out_ref[1:2] = (own_residual - next_step * image)[:, :params]

    for stage in range(5):
        block_wait_sent(stage)
    group_wait(ctx.at[pl.ds(0, groups - 1)], zsnd_sem, 0)
    for stage in range(2):
        group_wait(wide.at[stage, pl.ds(0, groups - 1)], zsnd_sem, 1 + stage)
    group_wait(row_snd.at[pl.ds(0, groups - 1)], zsnd_sem, 3)


def on_device(groups, owners, jacobians, destination, other_group, live_rows, damping, right_side):
    count, rows, width = jacobians.shape
    params = width // 2
    padded = (params + LANES - 1) // LANES * LANES
    vmem = pl.BlockSpec(memory_space=pltpu.VMEM)
    flat = jacobians.reshape(count * rows, width)
    operands = [flat, destination, other_group, live_rows, damping, right_side]
    out = pl.pallas_call(
        functools.partial(cg_kernel, groups, owners, count, rows, params),
        out_shape=(
            jax.ShapeDtypeStruct((2, params), F32),
        ),
        in_specs=[pl.BlockSpec(memory_space=pltpu.HBM)] * 6,
        out_specs=(vmem,),
        scratch_shapes=[
            pltpu.VMEM((count * rows, width), BF16),
            pltpu.VMEM((width, count * rows), BF16),
            pltpu.SMEM((count,), jnp.int32),
            pltpu.SMEM((count,), jnp.int32),
            pltpu.SMEM((count,), jnp.int32),
            pltpu.VMEM((1, params), F32),
            pltpu.VMEM((1, params), F32),
            pltpu.VMEM((owners * MSG, LANES), F32),
            pltpu.VMEM((2, groups * groups, LANES), F32),
            pltpu.VMEM((owners * MSG, TERMS), BF16),
            pltpu.VMEM((width // LANES * 16, owners * MSG), BF16),
            pltpu.VMEM((PANEL, owners * MSG), BF16),
            pltpu.VMEM((owners * MSG, PANEL), BF16),
            pltpu.VMEM((5, owners * MSG, LANES), BF16),
            pltpu.VMEM((5, owners * MSG, LANES), BF16),
            pltpu.VMEM((groups, 2, padded), F32),
            pltpu.VMEM((2, groups, 2 * groups, 3 * LANES), BF16),
            pltpu.VMEM((groups, 1, padded), F32),
            pltpu.VMEM((groups, 1, padded), F32),
            pltpu.SemaphoreType.DMA((count,)),
            pltpu.SemaphoreType.DMA((5,)),
            pltpu.SemaphoreType.DMA((5,)),
            pltpu.SemaphoreType.DMA((5, 2)),
            pltpu.SemaphoreType.DMA((4,)),
            pltpu.SemaphoreType.DMA((4,)),
        ],
        compiler_params=pltpu.CompilerParams(
            collective_id=0, has_side_effects=True, vmem_limit_bytes=40 * 1024 * 1024
        ),
    )(
        *[pltpu.with_memory_space_constraint(operand, pltpu.HBM) for operand in operands]
    )[0]
    return out[0:1], out[1:2]


def solution(mesh):
    placed = (
        P(("group", "block"), None, None),
        P(("group", "block")),
        P(("group", "block")),
        P(("group", "block")),
        P(("group", "block"), None),
        P(("group", "block"), None),
    )
    return jax.shard_map(
        functools.partial(on_device, mesh.shape["group"], mesh.shape["block"]),
        mesh=mesh,
        in_specs=placed,
        out_specs=(P(("group", "block"), None), P(("group", "block"), None)),
        check_vma=False,
    )
```

```python
import functools
import itertools

import jax
import jax.numpy as jnp
from jax import lax
from jax.experimental import pallas as pl
from jax.experimental.pallas import tpu as pltpu
from jax.sharding import PartitionSpec as P

LANES = 128
MSG = 16
TERMS = 256
PANEL = 96
F32 = jnp.float32
BF16 = jnp.bfloat16


def total(value):
    return jnp.sum(jnp.sum(value, axis=1, keepdims=True), axis=0, keepdims=True)


def iota(shape, dim):
    return lax.broadcasted_iota(jnp.int32, shape, dim)


def dot(left, right, contract=((1,), (0,))):
    return lax.dot_general(left, right, (contract, ((), ())), preferred_element_type=F32)


def block_dims(owners):
    return (4, 4, 2) if owners == 32 else (1, owners // 2, 2)


def distance(offset, dims):
    return sum(min(step, size - step) for step, size in zip(offset[:2], dims))


def peer_offsets(dims):
    offsets = list(itertools.product(*[range(size) for size in dims]))
    return sorted(offsets, key=lambda offset: (-distance(offset, dims), -offset[2]))


def opposite(offset, dims):
    return tuple((size - step) % size for step, size in zip(offset, dims))


def peer_at(me, offset, dims):
    x, y, core = me // (dims[1] * dims[2]), (me // dims[2]) % dims[1], me % dims[2]
    x, y, core = ((at + step) % size for at, step, size in zip((x, y, core), offset, dims))
    return (x * dims[1] + y) * dims[2] + core


def scalar_row(last, total_rows):
    spot = (iota((16, total_rows), 1) & (MSG - 1)) == last
    return jnp.where(spot & (iota((16, total_rows), 0) == 0), 1.0, 0.0).astype(BF16)


def cg_kernel(
    groups, owners, count, rows, params,
    jac_hbm, dest_hbm, other_hbm, live_hbm, damp_hbm, rhs_hbm,
    out_ref,
    jac, jac_t, dest_ref, other_ref, live_ref, damp_ref, rhs_ref,
    unpack, extras, term_map, input_map, panel_map, row_map, snd, rcv, ctx, wide, row_snd, row_rcv,
    jac_sem, in_sem, snd_sem, rcv_sem, zsnd_sem, zrcv_sem,
):
    me_g = lax.axis_index("group")
    me_b = lax.axis_index("block")
    width = jac.shape[1]
    tiles = (params + LANES - 1) // LANES
    padded = tiles * LANES
    kpad = 16
    raw = width // LANES
    total_rows = owners * MSG
    late = min(8, owners // 2)
    chunks = sorted({(0, late), (late, 2 * late), (2 * late, owners)} - {(owners, owners)})

    dims = block_dims(owners)
    offsets = peer_offsets(dims)
    peers = [peer_at(me_b, offset, dims) for offset in offsets]
    group_order = sorted(range(1, groups), key=lambda step: -min(step, groups - step))

    barrier = pltpu.get_barrier_semaphore()
    for step in group_order:
        pl.semaphore_signal(
            barrier,
            inc=1,
            device_id=((me_g + step) % groups, me_b),
            device_id_type=pl.DeviceIdType.MESH,
        )
    for peer in peers[:-1]:
        pl.semaphore_signal(
            barrier, inc=1, device_id=(me_g, peer), device_id_type=pl.DeviceIdType.MESH
        )

    def block_copy(k):
        part = pl.ds(k * rows, rows)
        return pltpu.make_async_copy(jac_hbm.at[part], jac.at[part], jac_sem.at[k])

    small = [
        pltpu.make_async_copy(source, target, in_sem.at[i])
        for i, (source, target) in enumerate(
            [
                (dest_hbm, dest_ref),
                (other_hbm, other_ref),
                (live_hbm, live_ref),
                (damp_hbm, damp_ref),
                (rhs_hbm, rhs_ref),
            ]
        )
    ]
    for copy in small:
        copy.start()
    for k in range(count):
        block_copy(k).start()

    def slot_part(slot):
        return pl.ds(slot * MSG, MSG)

    def block_send(stage, first, end):
        for slot in range(first, min(end, owners - 1)):
            there = offsets.index(opposite(offsets[slot], dims))
            pltpu.make_async_remote_copy(
                src_ref=snd.at[stage, slot_part(slot)],
                dst_ref=rcv.at[stage, slot_part(there)],
                send_sem=snd_sem.at[stage],
                recv_sem=rcv_sem.at[stage, 0 if there < late else 1],
                device_id=(me_g, peers[slot]),
                device_id_type=pl.DeviceIdType.MESH,
            ).start()

    def block_wait_near(stage):
        part = rcv.at[stage, pl.ds(late * MSG, (owners - 1 - late) * MSG)]
        pltpu.make_async_copy(part, part, rcv_sem.at[stage, 1]).wait()

    def block_wait_far(stage):
        part = rcv.at[stage, pl.ds(0, late * MSG)]
        pltpu.make_async_copy(part, part, rcv_sem.at[stage, 0]).wait()

    def block_wait_sent(stage):
        part = snd.at[stage, pl.ds(0, (owners - 1) * MSG)]
        pltpu.make_async_copy(part, part, snd_sem.at[stage]).wait()

    def group_send(stage, src_of, dst):
        for step in group_order:
            peer = (me_g + step) % groups
            pltpu.make_async_remote_copy(
                src_ref=src_of(peer),
                dst_ref=dst,
                send_sem=zsnd_sem.at[stage],
                recv_sem=zrcv_sem.at[stage],
                device_id=(peer, me_b),
                device_id_type=pl.DeviceIdType.MESH,
            ).start()

    def group_wait(part, sem, stage):
        pltpu.make_async_copy(part, part, sem.at[stage]).wait()

    for copy in small:
        copy.wait()

    half = params // LANES
    near = groups * tiles
    sub = iota((kpad, TERMS), 0)
    lane = iota((kpad, TERMS), 1)
    block_lane = lane & (kpad - 1)
    dest_col = jnp.full((kpad, TERMS), -1, jnp.int32)
    dest_row = jnp.full((kpad, TERMS), -1, jnp.int32)
    live_col = jnp.zeros((kpad, LANES), jnp.int32)
    other_col = jnp.zeros((kpad, LANES), jnp.int32)
    for k in range(count):
        dest_col = jnp.where(sub == k, dest_ref[k], dest_col)
        dest_row = jnp.where(block_lane == k, dest_ref[k], dest_row)
        live_col = jnp.where(sub[:, :LANES] == k, live_ref[k], live_col)
        other_col = jnp.where(sub[:, :LANES] == k, other_ref[k], other_col)
    same = jnp.where((dest_col == dest_row) & (dest_row >= 0), 1.0, 0.0)
    rank_row = jnp.sum(jnp.where(sub < block_lane, same, 0.0), axis=0, keepdims=True)
    rank_col = jnp.sum(jnp.where((lane < sub), same, 0.0), axis=1, keepdims=True)
    slot_peer = jnp.zeros((owners, TERMS), jnp.int32)
    for number, peer in enumerate(peers):
        slot_peer = jnp.where(iota((owners, TERMS), 0) == number, peer, slot_peer)
    hit = jnp.where(jnp.broadcast_to(dest_row[:1], (owners, TERMS)) == slot_peer, 1.0, 0.0)
    rank = jnp.broadcast_to(rank_row, (owners, TERMS))
    to_slot = jnp.concatenate(
        [hit, jnp.where(rank == 0.0, hit, 0.0), jnp.where(rank == 1.0, hit, 0.0)], axis=0
    ).astype(BF16)

    def segment(row):
        return jnp.where(row < tiles, 0, jnp.where(row < 2 * tiles, 1, jnp.where(row < 3 * tiles, 2, 0)))

    row_at = iota((total_rows, 3 * owners), 0)
    slot_at = iota((total_rows, 3 * owners), 1)
    spread = (
        jnp.where(
            (row_at >> 4) + owners * segment(row_at & (MSG - 1)) == slot_at, 1.0, 0.0
        )
    ).astype(BF16)
    row = iota((total_rows, TERMS), 0) & (MSG - 1)
    term_lane = iota((total_rows, TERMS), 1)
    tile = term_lane >> 4
    last = 3 * tiles
    wanted = jnp.where(row < tiles, row, jnp.where(row < 2 * tiles, row - tiles, row - 2 * tiles) + half)
    allowed = (row < last) & ((tile == wanted) | ((row < tiles) & (tile == raw + row)))
    terms_to_rows = jnp.where(allowed, dot(spread, to_slot), 0.0)
    terms_to_rows = jnp.where((row == last) & (term_lane == kpad - 1), 1.0, terms_to_rows)
    term_map[...] = terms_to_rows.astype(BF16)
    input_map[...] = terms_to_rows.T[: raw * kpad].astype(BF16)
    keep = jnp.concatenate(
        [
            jnp.where((sub[:, :LANES] == k) & (lane[:, :LANES] < live_col), 1.0, 0.0)
            for k in range(count)
        ],
        axis=1,
    )
    def panel_target(row, ids_a, ids_b):
        part = segment(row)
        far = jnp.where(part == 1, row - tiles, row - 2 * tiles) * groups + near
        far = far.astype(F32) + jnp.where(part == 1, ids_a, ids_b)
        home = (row * groups + me_g).astype(F32)
        return jnp.where(row == last, float(2 * near), jnp.where(row < tiles, home, far))

    others = other_col.astype(F32).astype(BF16)
    ids = dot(to_slot[owners:, :kpad], others)
    there = jnp.zeros((owners, LANES), jnp.int32)
    for number, offset in enumerate(offsets):
        place = offsets.index(opposite(offset, dims))
        there = jnp.where(iota((owners, LANES), 0) == number, place, there)
    slot_lane = iota((owners, LANES), 1)
    targets = panel_target(slot_lane & (MSG - 1), ids[:owners], ids[owners:])
    per_tile = LANES // MSG
    unpack[...] = jnp.zeros((total_rows, LANES), F32)
    unpack[pl.ds(last, owners, stride=MSG), :] = jnp.where(
        (slot_lane >> 4) == (there & (per_tile - 1)), targets, 0.0
    )

    def tiles_of(value, first, number):
        return [value[:, c * LANES : (c + 1) * LANES] for c in range(first, first + number)]

    def send_rows(stage, row_of, values, extra=None):
        for first, end in chunks:
            part = pl.ds(first * MSG, (end - first) * MSG)
            out = dot(row_of[part], values)
            out = (out if extra is None else out + extra[part]).astype(BF16)
            snd[stage, part] = out
            block_send(stage, first, end)
        rcv[stage, slot_part(owners - 1)] = out[-MSG:]

    def receive_rows(stage, map_ref):
        block_wait_near(stage)
        near_rows = pl.ds(late * MSG, total_rows - late * MSG)
        out = dot(map_ref[:, late * MSG :], rcv[stage, near_rows])
        block_wait_far(stage)
        return out + dot(map_ref[:, : late * MSG], rcv[stage, pl.ds(0, late * MSG)])

    def send_terms(stage, terms, last_row, extra=None):
        high = terms.astype(BF16)
        low = (terms[:, :padded] - high[:, :padded].astype(F32)).astype(BF16)
        parts = tiles_of(high, 0, raw)
        if last_row is not None:
            carrier = jnp.where(sub[:, :LANES] == kpad - 1, last_row, terms[:, :LANES])
            parts[0] = carrier.astype(BF16)
        parts += tiles_of(low, 0, tiles)
        blank = jnp.zeros((kpad, LANES), BF16)
        parts += [blank] * (TERMS // kpad - len(parts))
        send_rows(stage, term_map, jnp.concatenate(parts, axis=0), extra)

    wide_lane = iota((groups, padded), 1)
    wide_row = iota((groups, padded), 0)
    valid = wide_lane < params
    shift = params % LANES

    def receive_terms(stage):
        return panel_of(receive_rows(stage, panel_map))

    def panel_of(out):
        home = jnp.concatenate([out[c * groups : (c + 1) * groups] for c in range(tiles)], axis=1)
        far = jnp.concatenate(
            [out[near + c * groups : near + (c + 1) * groups] for c in range(tiles)], axis=1
        )
        panel = home + pltpu.roll(far, padded - shift, 1)
        return jnp.where(valid, panel, 0.0), out[2 * near : 2 * near + 1]

    def send_panel(stage, panel, last_row):
        parts = tiles_of(panel, 0, tiles) + tiles_of(pltpu.roll(panel, shift, 1), 0, tiles)
        parts.append(jnp.broadcast_to(last_row, (groups, LANES)))
        parts.append(jnp.zeros((PANEL - 2 * near - groups, LANES), F32))
        send_rows(stage, row_map, jnp.concatenate(parts, axis=0).astype(BF16))

    def receive_inputs(stage):
        out = receive_rows(stage, input_map)
        inputs = jnp.concatenate([out[t * kpad : (t + 1) * kpad] for t in range(raw)], axis=1)
        return inputs.astype(BF16)

    one = iota((1, LANES), 1)

    def split(value, first):
        high = value.astype(BF16).astype(F32)
        middle = (value - high).astype(BF16).astype(F32)
        low = value - high - middle
        out = jnp.where(one == first, high, 0.0) + jnp.where(one == first + 1, middle, 0.0)
        return out + jnp.where(one == first + 2, low, 0.0)

    def lanes_of(value):
        value = jnp.sum(value, axis=0, keepdims=True)
        folded = sum(tiles_of(value, 0, tiles)[1:], value[:, :LANES])
        folded = folded + pltpu.roll(folded, LANES // 2, 1)
        high = folded.astype(BF16).astype(F32)
        return jnp.where(one < LANES // 2, high, folded - high)

    def own_row(panel):
        return jnp.sum(jnp.where(wide_row == me_g, panel, 0.0), axis=0, keepdims=True)

    def sum_over_groups(stage, panel, scalar):
        high = panel.astype(BF16).astype(F32)
        low = own_row(panel - high)
        parts = tiles_of(low, 0, tiles)
        scalar = jnp.zeros((1, LANES), F32) if scalar is None else scalar
        first = scalar.astype(BF16).astype(F32)
        second = (scalar - first).astype(BF16).astype(F32)
        parts += [first, second, scalar - first - second]
        extra = jnp.concatenate(parts, axis=0)
        head = high[:, : 3 * LANES]
        tail = jnp.concatenate([high[:, 3 * LANES :], extra], axis=1)
        wide[stage, me_g] = jnp.concatenate([head, tail], axis=0).astype(BF16)
        group_send(1 + stage, lambda peer: wide.at[stage, me_g], wide.at[stage, me_g])

    def summed_groups(stage):
        group_wait(wide.at[stage, pl.ds(0, groups - 1)], zrcv_sem, 1 + stage)
        out = jnp.zeros((groups, padded), F32)
        for g in range(groups):
            part = wide[stage, g].astype(F32)
            out = out + jnp.concatenate([part[:groups], part[groups:, : 2 * LANES]], axis=1)
            extras[stage, g * groups : (g + 1) * groups] = part[groups:, 2 * LANES :]
        rest = [extras[stage, pl.ds(c, groups, stride=groups), :] for c in range(groups)]
        scalar = total(rest[tiles] + rest[tiles + 1] + rest[tiles + 2])
        return out + jnp.concatenate(rest[:tiles], axis=1), scalar

    sum_rows = []
    for k in range(count):
        block_copy(k).wait()
        block = jac[k * rows : (k + 1) * rows, :].astype(F32)
        live = iota((rows, width), 0) < live_ref[k]
        kept = jnp.where(live, block, 0.0)
        sum_rows.append(jnp.sum(kept * kept, axis=0, keepdims=True))
        jac_t[:, k * rows : (k + 1) * rows] = jac[k * rows : (k + 1) * rows, :].T
    sum_rows += [jnp.zeros((1, width), F32)] * (kpad - count)
    squares = jnp.concatenate(sum_rows, axis=0)

    ctx[me_g] = jnp.zeros((2, padded), F32)
    ctx[me_g, 0:1, 0:params] = damp_ref[...]
    ctx[me_g, 1:2, 0:params] = rhs_ref[...]
    pl.semaphore_wait(barrier, owners - 1 + groups - 1)
    send_terms(0, squares, None, unpack)
    group_send(0, lambda peer: ctx.at[me_g], ctx.at[me_g])
    decode_lane = iota((kpad, total_rows), 1)
    decode = jnp.where(
        ((decode_lane & (MSG - 1)) == last)
        & ((decode_lane >> 4) // per_tile == iota((kpad, total_rows), 0)),
        1.0,
        0.0,
    ).astype(BF16)
    panel_row = iota((groups, total_rows), 0).astype(F32)

    def decode_rows(first, end):
        got = rcv[0, first:end]
        decoded = dot(decode[:, first:end], got)
        target = jnp.concatenate(
            [
                jnp.broadcast_to(decoded[t : t + 1], (groups, LANES))
                for t in range((total_rows + LANES - 1) // LANES)
            ],
            axis=1,
        )[:, first:end]
        mapped = jnp.concatenate(
            [
                jnp.where(target == panel_row[:, first:end] + float(at), 1.0, 0.0)
                for at in range(0, LANES, groups)
            ],
            axis=0,
        )
        low_map = mapped[:PANEL].astype(BF16)
        panel_map[:, first:end] = low_map
        return mapped, dot(low_map, got)

    block_wait_near(0)
    near_map, near_out = decode_rows(late * MSG, total_rows)
    block_wait_far(0)
    far_map, far_out = decode_rows(0, late * MSG)
    panel, unused = panel_of(near_out + far_out)
    sum_over_groups(0, panel, None)
    rows_to_panel = jnp.concatenate([far_map, near_map], axis=1)
    row_map[...] = rows_to_panel.T[:, :PANEL].astype(BF16)
    group_wait(ctx.at[pl.ds(0, groups - 1)], zrcv_sem, 0)
    damping = jnp.concatenate([ctx[g, 0:1, :] for g in range(groups)], axis=0)
    right_side = jnp.concatenate([ctx[g, 1:2, :] for g in range(groups)], axis=0)
    summed, unused = summed_groups(0)
    diagonal = jnp.where(valid, damping + summed, 1.0)
    direction = right_side / diagonal

    send_panel(1, direction, lanes_of(right_side * direction))
    first_direction = own_row(direction)
    own_damping = own_row(damping)
    damped_direction = damping * direction
    damped = total(own_damping * first_direction * first_direction)
    inputs = receive_inputs(1)
    product = dot(inputs, jac_t[...])
    kept = product * keep
    projected = kept.astype(BF16)
    returned = dot(projected, jac[...])
    send_terms(2, returned, split(damped + total(kept * projected.astype(F32)), 0))
    scalars = dot(scalar_row(last, total_rows), rcv[1])[:1]
    norm = total(scalars)
    panel, scalars = receive_terms(2)
    sum_over_groups(1, panel, scalars)
    summed, curvature = summed_groups(1)
    step_size = norm / curvature
    residual = right_side - step_size * (damped_direction + summed)
    scaled = residual / diagonal

    send_panel(3, scaled, lanes_of(residual * scaled))
    own_scaled = own_row(scaled)
    own_residual = own_row(residual)
    inputs = receive_inputs(3)
    next_norm = total(dot(scalar_row(last, total_rows), rcv[3])[:1])
    beta = next_norm / norm
    product = dot(inputs, jac_t[...]) + beta * product
    kept = product * keep
    projected = kept.astype(BF16)
    returned = dot(projected, jac[...])
    next_direction = own_scaled + beta * first_direction
    partial = total(kept * projected.astype(F32)) + total(
        own_damping * next_direction * next_direction
    )
    send_terms(4, returned, split(partial, 0))
    for stage in range(4):
        block_wait_sent(stage)
    group_wait(ctx.at[pl.ds(0, groups - 1)], zsnd_sem, 0)
    for stage in range(2):
        group_wait(wide.at[stage, pl.ds(0, groups - 1)], zsnd_sem, 1 + stage)
    panel, scalars = receive_terms(4)
    spare = jnp.concatenate([scalars] * tiles, axis=1)
    spare = pltpu.roll(spare, shift, 1)
    panel = jnp.where(valid, panel, jnp.broadcast_to(spare, panel.shape))
    for g in range(groups):
        row_snd[g] = panel[g : g + 1]
    row_rcv[me_g] = own_row(panel)
    group_send(3, lambda peer: row_snd.at[peer], row_rcv.at[me_g])
    block_wait_sent(4)
    group_wait(row_snd.at[pl.ds(0, groups - 1)], zsnd_sem, 3)
    group_wait(row_rcv.at[pl.ds(0, groups - 1)], zrcv_sem, 3)
    out = row_rcv[0]
    for g in range(1, groups):
        out = out + row_rcv[g]
    one_lane = iota((1, padded), 1)
    curvature = total(jnp.where(one_lane < params, 0.0, out))
    next_step = next_norm / curvature
    image = own_damping * next_direction + out
    out_ref[0:1] = (step_size * first_direction + next_step * next_direction)[:, :params]
    out_ref[1:2] = (own_residual - next_step * image)[:, :params]


def on_device(groups, owners, jacobians, destination, other_group, live_rows, damping, right_side):
    count, rows, width = jacobians.shape
    params = width // 2
    padded = (params + LANES - 1) // LANES * LANES
    vmem = pl.BlockSpec(memory_space=pltpu.VMEM)
    flat = jacobians.reshape(count * rows, width)
    operands = [flat, destination, other_group, live_rows, damping, right_side]
    out = pl.pallas_call(
        functools.partial(cg_kernel, groups, owners, count, rows, params),
        out_shape=(
            jax.ShapeDtypeStruct((2, params), F32),
        ),
        in_specs=[pl.BlockSpec(memory_space=pltpu.HBM)] * 6,
        out_specs=(vmem,),
        scratch_shapes=[
            pltpu.VMEM((count * rows, width), BF16),
            pltpu.VMEM((width, count * rows), BF16),
            pltpu.SMEM((count,), jnp.int32),
            pltpu.SMEM((count,), jnp.int32),
            pltpu.SMEM((count,), jnp.int32),
            pltpu.VMEM((1, params), F32),
            pltpu.VMEM((1, params), F32),
            pltpu.VMEM((owners * MSG, LANES), F32),
            pltpu.VMEM((2, groups * groups, LANES), F32),
            pltpu.VMEM((owners * MSG, TERMS), BF16),
            pltpu.VMEM((width // LANES * 16, owners * MSG), BF16),
            pltpu.VMEM((PANEL, owners * MSG), BF16),
            pltpu.VMEM((owners * MSG, PANEL), BF16),
            pltpu.VMEM((5, owners * MSG, LANES), BF16),
            pltpu.VMEM((5, owners * MSG, LANES), BF16),
            pltpu.VMEM((groups, 2, padded), F32),
            pltpu.VMEM((2, groups, 2 * groups, 3 * LANES), BF16),
            pltpu.VMEM((groups, 1, padded), F32),
            pltpu.VMEM((groups, 1, padded), F32),
            pltpu.SemaphoreType.DMA((count,)),
            pltpu.SemaphoreType.DMA((5,)),
            pltpu.SemaphoreType.DMA((5,)),
            pltpu.SemaphoreType.DMA((5, 2)),
            pltpu.SemaphoreType.DMA((4,)),
            pltpu.SemaphoreType.DMA((4,)),
        ],
        compiler_params=pltpu.CompilerParams(
            collective_id=0, has_side_effects=True, vmem_limit_bytes=40 * 1024 * 1024
        ),
    )(
        *[pltpu.with_memory_space_constraint(operand, pltpu.HBM) for operand in operands]
    )[0]
    return out[0:1], out[1:2]


def solution(mesh):
    placed = (
        P(("group", "block"), None, None),
        P(("group", "block")),
        P(("group", "block")),
        P(("group", "block")),
        P(("group", "block"), None),
        P(("group", "block"), None),
    )
    return jax.shard_map(
        functools.partial(on_device, mesh.shape["group"], mesh.shape["block"]),
        mesh=mesh,
        in_specs=placed,
        out_specs=(P(("group", "block"), None), P(("group", "block"), None)),
        check_vma=False,
    )
```

```python
import functools
import itertools

import jax
import jax.numpy as jnp
from jax import lax
from jax.experimental import pallas as pl
from jax.experimental.pallas import tpu as pltpu
from jax.sharding import PartitionSpec as P

LANES = 128
MSG = 16
TERMS = 256
PANEL = 96
F32 = jnp.float32
BF16 = jnp.bfloat16


def total(value):
    return jnp.sum(jnp.sum(value, axis=1, keepdims=True), axis=0, keepdims=True)


def iota(shape, dim):
    return lax.broadcasted_iota(jnp.int32, shape, dim)


def dot(left, right, contract=((1,), (0,))):
    return lax.dot_general(left, right, (contract, ((), ())), preferred_element_type=F32)


def block_dims(owners):
    return (4, 4, 2) if owners == 32 else (1, owners // 2, 2)


def distance(offset, dims):
    return sum(min(step, size - step) for step, size in zip(offset[:2], dims))


def peer_offsets(dims):
    offsets = list(itertools.product(*[range(size) for size in dims]))
    return sorted(offsets, key=lambda offset: (-distance(offset, dims), -offset[2]))


def opposite(offset, dims):
    return tuple((size - step) % size for step, size in zip(offset, dims))


def peer_at(me, offset, dims):
    x, y, core = me // (dims[1] * dims[2]), (me // dims[2]) % dims[1], me % dims[2]
    x, y, core = ((at + step) % size for at, step, size in zip((x, y, core), offset, dims))
    return (x * dims[1] + y) * dims[2] + core


def scalar_row(last, total_rows):
    spot = (iota((16, total_rows), 1) & (MSG - 1)) == last
    return jnp.where(spot & (iota((16, total_rows), 0) == 0), 1.0, 0.0).astype(BF16)


def cg_kernel(
    groups, owners, count, rows, params,
    jac_hbm, dest_hbm, other_hbm, live_hbm, damp_hbm, rhs_hbm,
    out_ref,
    jac, jac_t, dest_ref, other_ref, live_ref, damp_ref, rhs_ref,
    unpack, extras, term_map, input_map, panel_map, row_map, snd, rcv, ctx, wide, row_snd, row_rcv,
    jac_sem, in_sem, snd_sem, rcv_sem, zsnd_sem, zrcv_sem,
):
    me_g = lax.axis_index("group")
    me_b = lax.axis_index("block")
    width = jac.shape[1]
    tiles = (params + LANES - 1) // LANES
    padded = tiles * LANES
    kpad = 16
    raw = width // LANES
    total_rows = owners * MSG
    late = min(8, owners // 2)
    chunks = sorted({(0, late), (late, 2 * late), (2 * late, owners)} - {(owners, owners)})

    dims = block_dims(owners)
    offsets = peer_offsets(dims)
    peers = [peer_at(me_b, offset, dims) for offset in offsets]
    group_order = sorted(range(1, groups), key=lambda step: -min(step, groups - step))

    barrier = pltpu.get_barrier_semaphore()
    for step in group_order:
        pl.semaphore_signal(
            barrier,
            inc=1,
            device_id=((me_g + step) % groups, me_b),
            device_id_type=pl.DeviceIdType.MESH,
        )
    for peer in peers[:-1]:
        pl.semaphore_signal(
            barrier, inc=1, device_id=(me_g, peer), device_id_type=pl.DeviceIdType.MESH
        )

    def block_copy(k):
        part = pl.ds(k * rows, rows)
        return pltpu.make_async_copy(jac_hbm.at[part], jac.at[part], jac_sem.at[k])

    small = [
        pltpu.make_async_copy(source, target, in_sem.at[i])
        for i, (source, target) in enumerate(
            [
                (dest_hbm, dest_ref),
                (other_hbm, other_ref),
                (live_hbm, live_ref),
                (damp_hbm, damp_ref),
                (rhs_hbm, rhs_ref),
            ]
        )
    ]
    for copy in small:
        copy.start()
    for k in range(count):
        block_copy(k).start()

    def slot_part(slot):
        return pl.ds(slot * MSG, MSG)

    def block_send(stage, first, end):
        for slot in range(first, min(end, owners - 1)):
            there = offsets.index(opposite(offsets[slot], dims))
            pltpu.make_async_remote_copy(
                src_ref=snd.at[stage, slot_part(slot)],
                dst_ref=rcv.at[stage, slot_part(there)],
                send_sem=snd_sem.at[stage],
                recv_sem=rcv_sem.at[stage, 0 if there < late else 1],
                device_id=(me_g, peers[slot]),
                device_id_type=pl.DeviceIdType.MESH,
            ).start()

    def block_wait_near(stage):
        part = rcv.at[stage, pl.ds(late * MSG, (owners - 1 - late) * MSG)]
        pltpu.make_async_copy(part, part, rcv_sem.at[stage, 1]).wait()

    def block_wait_far(stage):
        part = rcv.at[stage, pl.ds(0, late * MSG)]
        pltpu.make_async_copy(part, part, rcv_sem.at[stage, 0]).wait()

    def block_wait_sent(stage):
        part = snd.at[stage, pl.ds(0, (owners - 1) * MSG)]
        pltpu.make_async_copy(part, part, snd_sem.at[stage]).wait()

    def group_send(stage, src_of, dst, far_sem=None):
        for step in group_order:
            peer = (me_g + step) % groups
            pltpu.make_async_remote_copy(
                src_ref=src_of(peer),
                dst_ref=dst,
                send_sem=zsnd_sem.at[stage],
                recv_sem=zrcv_sem.at[far_sem if far_sem and is_far(step) else stage],
                device_id=(peer, me_b),
                device_id_type=pl.DeviceIdType.MESH,
            ).start()

    def is_far(step):
        return min(step, groups - step) > groups // 4

    def group_wait(part, sem, stage):
        pltpu.make_async_copy(part, part, sem.at[stage]).wait()

    for copy in small:
        copy.wait()

    half = params // LANES
    near = groups * tiles
    sub = iota((kpad, TERMS), 0)
    lane = iota((kpad, TERMS), 1)
    block_lane = lane & (kpad - 1)
    dest_col = jnp.full((kpad, TERMS), -1, jnp.int32)
    dest_row = jnp.full((kpad, TERMS), -1, jnp.int32)
    live_col = jnp.zeros((kpad, LANES), jnp.int32)
    other_col = jnp.zeros((kpad, LANES), jnp.int32)
    for k in range(count):
        dest_col = jnp.where(sub == k, dest_ref[k], dest_col)
        dest_row = jnp.where(block_lane == k, dest_ref[k], dest_row)
        live_col = jnp.where(sub[:, :LANES] == k, live_ref[k], live_col)
        other_col = jnp.where(sub[:, :LANES] == k, other_ref[k], other_col)
    same = jnp.where((dest_col == dest_row) & (dest_row >= 0), 1.0, 0.0)
    rank_row = jnp.sum(jnp.where(sub < block_lane, same, 0.0), axis=0, keepdims=True)
    rank_col = jnp.sum(jnp.where((lane < sub), same, 0.0), axis=1, keepdims=True)
    slot_peer = jnp.zeros((owners, TERMS), jnp.int32)
    for number, peer in enumerate(peers):
        slot_peer = jnp.where(iota((owners, TERMS), 0) == number, peer, slot_peer)
    hit = jnp.where(jnp.broadcast_to(dest_row[:1], (owners, TERMS)) == slot_peer, 1.0, 0.0)
    rank = jnp.broadcast_to(rank_row, (owners, TERMS))
    to_slot = jnp.concatenate(
        [hit, jnp.where(rank == 0.0, hit, 0.0), jnp.where(rank == 1.0, hit, 0.0)], axis=0
    ).astype(BF16)

    def segment(row):
        return jnp.where(row < tiles, 0, jnp.where(row < 2 * tiles, 1, jnp.where(row < 3 * tiles, 2, 0)))

    row_at = iota((total_rows, 3 * owners), 0)
    slot_at = iota((total_rows, 3 * owners), 1)
    spread = (
        jnp.where(
            (row_at >> 4) + owners * segment(row_at & (MSG - 1)) == slot_at, 1.0, 0.0
        )
    ).astype(BF16)
    row = iota((total_rows, TERMS), 0) & (MSG - 1)
    term_lane = iota((total_rows, TERMS), 1)
    tile = term_lane >> 4
    last = 3 * tiles
    wanted = jnp.where(row < tiles, row, jnp.where(row < 2 * tiles, row - tiles, row - 2 * tiles) + half)
    allowed = (row < last) & ((tile == wanted) | ((row < tiles) & (tile == raw + row)))
    terms_to_rows = jnp.where(allowed, dot(spread, to_slot), 0.0)
    terms_to_rows = jnp.where((row == last) & (term_lane == kpad - 1), 1.0, terms_to_rows)
    term_map[...] = terms_to_rows.astype(BF16)
    input_map[...] = terms_to_rows.T[: raw * kpad].astype(BF16)
    keep = jnp.concatenate(
        [
            jnp.where((sub[:, :LANES] == k) & (lane[:, :LANES] < live_col), 1.0, 0.0)
            for k in range(count)
        ],
        axis=1,
    )
    def panel_target(row, ids_a, ids_b):
        part = segment(row)
        far = jnp.where(part == 1, row - tiles, row - 2 * tiles) * groups + near
        far = far.astype(F32) + jnp.where(part == 1, ids_a, ids_b)
        home = (row * groups + me_g).astype(F32)
        return jnp.where(row == last, float(2 * near), jnp.where(row < tiles, home, far))

    others = other_col.astype(F32).astype(BF16)
    ids = dot(to_slot[owners:, :kpad], others)
    there = jnp.zeros((owners, LANES), jnp.int32)
    for number, offset in enumerate(offsets):
        place = offsets.index(opposite(offset, dims))
        there = jnp.where(iota((owners, LANES), 0) == number, place, there)
    slot_lane = iota((owners, LANES), 1)
    targets = panel_target(slot_lane & (MSG - 1), ids[:owners], ids[owners:])
    per_tile = LANES // MSG
    unpack[...] = jnp.zeros((total_rows, LANES), F32)
    unpack[pl.ds(last, owners, stride=MSG), :] = jnp.where(
        (slot_lane >> 4) == (there & (per_tile - 1)), targets, 0.0
    )

    def tiles_of(value, first, number):
        return [value[:, c * LANES : (c + 1) * LANES] for c in range(first, first + number)]

    def send_rows(stage, row_of, values, extra=None):
        for first, end in chunks:
            part = pl.ds(first * MSG, (end - first) * MSG)
            out = dot(row_of[part], values)
            out = (out if extra is None else out + extra[part]).astype(BF16)
            snd[stage, part] = out
            block_send(stage, first, end)
        rcv[stage, slot_part(owners - 1)] = out[-MSG:]

    def receive_rows(stage, map_ref):
        block_wait_near(stage)
        near_rows = pl.ds(late * MSG, total_rows - late * MSG)
        out = dot(map_ref[:, late * MSG :], rcv[stage, near_rows])
        block_wait_far(stage)
        return out + dot(map_ref[:, : late * MSG], rcv[stage, pl.ds(0, late * MSG)])

    def send_terms(stage, terms, last_row, extra=None):
        high = terms.astype(BF16)
        low = (terms[:, :padded] - high[:, :padded].astype(F32)).astype(BF16)
        parts = tiles_of(high, 0, raw)
        if last_row is not None:
            carrier = jnp.where(sub[:, :LANES] == kpad - 1, last_row, terms[:, :LANES])
            parts[0] = carrier.astype(BF16)
        parts += tiles_of(low, 0, tiles)
        blank = jnp.zeros((kpad, LANES), BF16)
        parts += [blank] * (TERMS // kpad - len(parts))
        send_rows(stage, term_map, jnp.concatenate(parts, axis=0), extra)

    wide_lane = iota((groups, padded), 1)
    wide_row = iota((groups, padded), 0)
    valid = wide_lane < params
    shift = params % LANES

    def receive_terms(stage):
        return panel_of(receive_rows(stage, panel_map))

    def panel_of(out):
        home = jnp.concatenate([out[c * groups : (c + 1) * groups] for c in range(tiles)], axis=1)
        far = jnp.concatenate(
            [out[near + c * groups : near + (c + 1) * groups] for c in range(tiles)], axis=1
        )
        panel = home + pltpu.roll(far, padded - shift, 1)
        return jnp.where(valid, panel, 0.0), out[2 * near : 2 * near + 1]

    def send_panel(stage, panel, last_row):
        parts = tiles_of(panel, 0, tiles) + tiles_of(pltpu.roll(panel, shift, 1), 0, tiles)
        parts.append(jnp.broadcast_to(last_row, (groups, LANES)))
        parts.append(jnp.zeros((PANEL - 2 * near - groups, LANES), F32))
        send_rows(stage, row_map, jnp.concatenate(parts, axis=0).astype(BF16))

    def receive_inputs(stage):
        out = receive_rows(stage, input_map)
        inputs = jnp.concatenate([out[t * kpad : (t + 1) * kpad] for t in range(raw)], axis=1)
        return inputs.astype(BF16)

    one = iota((1, LANES), 1)

    def split(value, first):
        high = value.astype(BF16).astype(F32)
        middle = (value - high).astype(BF16).astype(F32)
        low = value - high - middle
        out = jnp.where(one == first, high, 0.0) + jnp.where(one == first + 1, middle, 0.0)
        return out + jnp.where(one == first + 2, low, 0.0)

    def lanes_of(value):
        value = jnp.sum(value, axis=0, keepdims=True)
        folded = sum(tiles_of(value, 0, tiles)[1:], value[:, :LANES])
        folded = folded + pltpu.roll(folded, LANES // 2, 1)
        high = folded.astype(BF16).astype(F32)
        return jnp.where(one < LANES // 2, high, folded - high)

    def own_row(panel):
        return jnp.sum(jnp.where(wide_row == me_g, panel, 0.0), axis=0, keepdims=True)

    def sum_over_groups(stage, panel, scalar):
        high = panel.astype(BF16).astype(F32)
        low = own_row(panel - high)
        parts = tiles_of(low, 0, tiles)
        scalar = jnp.zeros((1, LANES), F32) if scalar is None else scalar
        first = scalar.astype(BF16).astype(F32)
        second = (scalar - first).astype(BF16).astype(F32)
        parts += [first, second, scalar - first - second]
        extra = jnp.concatenate(parts, axis=0)
        head = high[:, : 3 * LANES]
        tail = jnp.concatenate([high[:, 3 * LANES :], extra], axis=1)
        wide[stage, me_g] = jnp.concatenate([head, tail], axis=0).astype(BF16)
        group_send(1 + stage, lambda peer: wide.at[stage, me_g], wide.at[stage, me_g], 4 + stage)

    def summed_groups(stage):
        far_steps = [step for step in range(1, groups) if is_far(step)]
        near_steps = [step for step in range(groups) if not is_far(step)]
        out = jnp.zeros((groups, padded), F32)
        for steps, sem, number in (
            (near_steps, 1 + stage, len(near_steps) - 1),
            (far_steps, 4 + stage, len(far_steps)),
        ):
            group_wait(wide.at[stage, pl.ds(0, number)], zrcv_sem, sem)
            for step in steps:
                g = (me_g + step) % groups
                part = wide[stage, g].astype(F32)
                out = out + jnp.concatenate([part[:groups], part[groups:, : 2 * LANES]], axis=1)
                place = pl.ds(pl.multiple_of(g * groups, groups), groups)
                extras[stage, place] = part[groups:, 2 * LANES :]
        rest = [extras[stage, pl.ds(c, groups, stride=groups), :] for c in range(groups)]
        scalar = total(rest[tiles] + rest[tiles + 1] + rest[tiles + 2])
        return out + jnp.concatenate(rest[:tiles], axis=1), scalar

    sum_rows = []
    for k in range(count):
        block_copy(k).wait()
        block = jac[k * rows : (k + 1) * rows, :].astype(F32)
        live = iota((rows, width), 0) < live_ref[k]
        kept = jnp.where(live, block, 0.0)
        sum_rows.append(jnp.sum(kept * kept, axis=0, keepdims=True))
        jac_t[:, k * rows : (k + 1) * rows] = jac[k * rows : (k + 1) * rows, :].T
    sum_rows += [jnp.zeros((1, width), F32)] * (kpad - count)
    squares = jnp.concatenate(sum_rows, axis=0)

    ctx[me_g] = jnp.zeros((2, padded), F32)
    ctx[me_g, 0:1, 0:params] = damp_ref[...]
    ctx[me_g, 1:2, 0:params] = rhs_ref[...]
    pl.semaphore_wait(barrier, owners - 1 + groups - 1)
    send_terms(0, squares, None, unpack)
    group_send(0, lambda peer: ctx.at[me_g], ctx.at[me_g])
    decode_lane = iota((kpad, total_rows), 1)
    decode = jnp.where(
        ((decode_lane & (MSG - 1)) == last)
        & ((decode_lane >> 4) // per_tile == iota((kpad, total_rows), 0)),
        1.0,
        0.0,
    ).astype(BF16)
    panel_row = iota((groups, total_rows), 0).astype(F32)

    def decode_rows(first, end):
        got = rcv[0, first:end]
        decoded = dot(decode[:, first:end], got)
        target = jnp.concatenate(
            [
                jnp.broadcast_to(decoded[t : t + 1], (groups, LANES))
                for t in range((total_rows + LANES - 1) // LANES)
            ],
            axis=1,
        )[:, first:end]
        mapped = jnp.concatenate(
            [
                jnp.where(target == panel_row[:, first:end] + float(at), 1.0, 0.0)
                for at in range(0, LANES, groups)
            ],
            axis=0,
        )
        low_map = mapped[:PANEL].astype(BF16)
        panel_map[:, first:end] = low_map
        return mapped, dot(low_map, got)

    block_wait_near(0)
    near_map, near_out = decode_rows(late * MSG, total_rows)
    block_wait_far(0)
    far_map, far_out = decode_rows(0, late * MSG)
    panel, unused = panel_of(near_out + far_out)
    sum_over_groups(0, panel, None)
    rows_to_panel = jnp.concatenate([far_map, near_map], axis=1)
    row_map[...] = rows_to_panel.T[:, :PANEL].astype(BF16)
    group_wait(ctx.at[pl.ds(0, groups - 1)], zrcv_sem, 0)
    damping = jnp.concatenate([ctx[g, 0:1, :] for g in range(groups)], axis=0)
    right_side = jnp.concatenate([ctx[g, 1:2, :] for g in range(groups)], axis=0)
    summed, unused = summed_groups(0)
    diagonal = jnp.where(valid, damping + summed, 1.0)
    direction = right_side / diagonal

    send_panel(1, direction, lanes_of(right_side * direction))
    first_direction = own_row(direction)
    own_damping = own_row(damping)
    damped_direction = damping * direction
    damped = total(own_damping * first_direction * first_direction)
    inputs = receive_inputs(1)
    product = dot(inputs, jac_t[...])
    kept = product * keep
    projected = kept.astype(BF16)
    returned = dot(projected, jac[...])
    send_terms(2, returned, split(damped + total(kept * projected.astype(F32)), 0))
    scalars = dot(scalar_row(last, total_rows), rcv[1])[:1]
    norm = total(scalars)
    panel, scalars = receive_terms(2)
    sum_over_groups(1, panel, scalars)
    summed, curvature = summed_groups(1)
    step_size = norm / curvature
    residual = right_side - step_size * (damped_direction + summed)
    scaled = residual / diagonal

    send_panel(3, scaled, lanes_of(residual * scaled))
    own_scaled = own_row(scaled)
    own_residual = own_row(residual)
    inputs = receive_inputs(3)
    next_norm = total(dot(scalar_row(last, total_rows), rcv[3])[:1])
    beta = next_norm / norm
    product = dot(inputs, jac_t[...]) + beta * product
    kept = product * keep
    projected = kept.astype(BF16)
    returned = dot(projected, jac[...])
    next_direction = own_scaled + beta * first_direction
    partial = total(kept * projected.astype(F32)) + total(
        own_damping * next_direction * next_direction
    )
    send_terms(4, returned, split(partial, 0))
    for stage in range(4):
        block_wait_sent(stage)
    group_wait(ctx.at[pl.ds(0, groups - 1)], zsnd_sem, 0)
    for stage in range(2):
        group_wait(wide.at[stage, pl.ds(0, groups - 1)], zsnd_sem, 1 + stage)
    panel, scalars = receive_terms(4)
    spare = jnp.concatenate([scalars] * tiles, axis=1)
    spare = pltpu.roll(spare, shift, 1)
    panel = jnp.where(valid, panel, jnp.broadcast_to(spare, panel.shape))
    for g in range(groups):
        row_snd[g] = panel[g : g + 1]
    row_rcv[me_g] = own_row(panel)
    group_send(3, lambda peer: row_snd.at[peer], row_rcv.at[me_g])
    block_wait_sent(4)
    group_wait(row_snd.at[pl.ds(0, groups - 1)], zsnd_sem, 3)
    group_wait(row_rcv.at[pl.ds(0, groups - 1)], zrcv_sem, 3)
    out = row_rcv[0]
    for g in range(1, groups):
        out = out + row_rcv[g]
    one_lane = iota((1, padded), 1)
    curvature = total(jnp.where(one_lane < params, 0.0, out))
    next_step = next_norm / curvature
    image = own_damping * next_direction + out
    out_ref[0:1] = (step_size * first_direction + next_step * next_direction)[:, :params]
    out_ref[1:2] = (own_residual - next_step * image)[:, :params]


def on_device(groups, owners, jacobians, destination, other_group, live_rows, damping, right_side):
    count, rows, width = jacobians.shape
    params = width // 2
    padded = (params + LANES - 1) // LANES * LANES
    vmem = pl.BlockSpec(memory_space=pltpu.VMEM)
    flat = jacobians.reshape(count * rows, width)
    operands = [flat, destination, other_group, live_rows, damping, right_side]
    out = pl.pallas_call(
        functools.partial(cg_kernel, groups, owners, count, rows, params),
        out_shape=(
            jax.ShapeDtypeStruct((2, params), F32),
        ),
        in_specs=[pl.BlockSpec(memory_space=pltpu.HBM)] * 6,
        out_specs=(vmem,),
        scratch_shapes=[
            pltpu.VMEM((count * rows, width), BF16),
            pltpu.VMEM((width, count * rows), BF16),
            pltpu.SMEM((count,), jnp.int32),
            pltpu.SMEM((count,), jnp.int32),
            pltpu.SMEM((count,), jnp.int32),
            pltpu.VMEM((1, params), F32),
            pltpu.VMEM((1, params), F32),
            pltpu.VMEM((owners * MSG, LANES), F32),
            pltpu.VMEM((2, groups * groups, LANES), F32),
            pltpu.VMEM((owners * MSG, TERMS), BF16),
            pltpu.VMEM((width // LANES * 16, owners * MSG), BF16),
            pltpu.VMEM((PANEL, owners * MSG), BF16),
            pltpu.VMEM((owners * MSG, PANEL), BF16),
            pltpu.VMEM((5, owners * MSG, LANES), BF16),
            pltpu.VMEM((5, owners * MSG, LANES), BF16),
            pltpu.VMEM((groups, 2, padded), F32),
            pltpu.VMEM((2, groups, 2 * groups, 3 * LANES), BF16),
            pltpu.VMEM((groups, 1, padded), F32),
            pltpu.VMEM((groups, 1, padded), F32),
            pltpu.SemaphoreType.DMA((count,)),
            pltpu.SemaphoreType.DMA((5,)),
            pltpu.SemaphoreType.DMA((5,)),
            pltpu.SemaphoreType.DMA((5, 2)),
            pltpu.SemaphoreType.DMA((4,)),
            pltpu.SemaphoreType.DMA((6,)),
        ],
        compiler_params=pltpu.CompilerParams(
            collective_id=0, has_side_effects=True, vmem_limit_bytes=40 * 1024 * 1024
        ),
    )(
        *[pltpu.with_memory_space_constraint(operand, pltpu.HBM) for operand in operands]
    )[0]
    return out[0:1], out[1:2]


def solution(mesh):
    placed = (
        P(("group", "block"), None, None),
        P(("group", "block")),
        P(("group", "block")),
        P(("group", "block")),
        P(("group", "block"), None),
        P(("group", "block"), None),
    )
    return jax.shard_map(
        functools.partial(on_device, mesh.shape["group"], mesh.shape["block"]),
        mesh=mesh,
        in_specs=placed,
        out_specs=(P(("group", "block"), None), P(("group", "block"), None)),
        check_vma=False,
    )
```
